256 devices in a mesh: cache: 32 (over x, z), tensor: 8 (over y, core).
Axes of the slice: x: 4, y: 4, z: 8, core: 2. Of those that a mesh axis runs over, the one named last changes fastest.
Arguments:
- queries: bfloat16 [1024, 32, 8192], P('cache', None, 'tensor'), may hold values from -18 to 18
- prefix_kv: bfloat16 [2, 32, 512, 1024], P(None, 'cache', None, 'tensor'), may hold values from -12 to 12
- suffix_kv: bfloat16 [2, 1024, 32, 1024], P(None, 'cache', None, 'tensor'), may hold values from -12 to 12
- candidate_prefix: int32 [1024, 1], P('cache'), may hold values from 0 to 31; in each aligned block of 32 rows (0 to 31, 32 to 63, ...) at most 2 rows name the same one
- w_out: bfloat16 [8192, 4096], P('tensor'), may hold values from -1 to 1
Outputs:
- projected: bfloat16 [1024, 32, 4096], P('cache', None, 'tensor')
The draws below stay inside these ranges and needn't reach their ends.
Inputs may be any that keep to these rules, and one draw needn't show every extreme that they name: `candidate_prefix`: the passage with id p has its cache at prefix_kv[:, p]. Among the candidates of one index of cache at most 2 name the same passage, and exactly 2 do for some passage in some of them.
All inputs are finite; a program needn't handle non-finite values.
Results may differ from the reference program's by a relative error of at most 0.019.
Values may be sent and summed in bfloat16 or wider, within the bound.
No kernel may reach another device: no remote copies, remote signals or barrier semaphores. Data moves between devices by JAX's collectives and lax.ppermute only.
A program may use at most 128 MiB of HBM per device.

```python
import math
import jax
import jax.numpy as jnp
import numpy as np
from jax import lax

H = 64
KVH = 8
HD = 128
DOUT = 4096
SUF = 32
L = 512
CAND_DEV = 32
CANDS = 1024
NPREFIX = 32
CAP = 2
N_CACHE = 32


def draw_queries(key, part):
    key = jax.random.fold_in(key, 11)
    first = jax.random.fold_in(key, 0)
    full_shape = (CANDS, SUF, H * HD)
    result = 1.5 * jax.random.truncated_normal(first, -4.0, 4.0, full_shape, jnp.float32)
    return result.astype(jnp.bfloat16)


def draw_prefix_kv(key, part):
    key = jax.random.fold_in(key, 23)
    first = jax.random.fold_in(key, 0)
    full_shape = (2, NPREFIX, L, KVH * HD)
    result = jax.random.truncated_normal(first, -4.0, 4.0, full_shape, jnp.float32)
    return result.astype(jnp.bfloat16)


def draw_suffix_kv(key, part):
    key = jax.random.fold_in(key, 37)
    first = jax.random.fold_in(key, 0)
    full_shape = (2, CANDS, SUF, KVH * HD)
    leading = (jnp.arange(2) == 0)[:, None, None, None]
    factor = jnp.where(leading, 1.3, 1.0)
    result = factor * jax.random.truncated_normal(first, -4.0, 4.0, full_shape, jnp.float32)
    return result.astype(jnp.bfloat16)


def with_spikes(values, rng, source, target, shards_of, factor):
    owner, partner = [(jnp.arange(values.shape[axis_at]) // (values.shape[axis_at] // shards_of)).reshape([-1 if axis == axis_at else 1 for axis in range(values.ndim)]) for axis_at in (source, target)]
    chosen = jax.random.permutation(rng, shards_of)[partner]
    strong = (owner == chosen) | (owner == (partner + shards_of // 2) % shards_of)
    return jnp.where(strong, factor * values, values)


def steps_of(key, dims, shards, smallest, largest):
    loudness, own = 1.0, jax.random.fold_in(key, 6)
    for axis_at, shards_of in shards:
        heights = jnp.exp(jax.random.uniform(jax.random.fold_in(own, axis_at), (shards_of,), jnp.float32, smallest / len(shards), largest / len(shards)))
        loudness = loudness * jnp.repeat(heights, dims[axis_at] // shards_of).reshape([-1 if axis == axis_at else 1 for axis in range(len(dims))])
    return loudness


def routed_block(rng, own, number, rows, count, top, bound, lean):
    order = jax.random.permutation(rng, count)
    packed, ordinary = portions_of(count, rows * top, bound, lean, True), portions_of(count, rows * top, bound, lean, False)
    places = jnp.arange(count)

    def named(lengths, turn):
        used = int((lengths > 0).sum())
        fixed = max(1, used // 4)
        passed = fixed + (places - fixed + turn * (used - fixed)) % max(1, count - fixed)
        return jnp.zeros((count,), jnp.int32).at[order[jnp.where(places < fixed, places, passed)]].set(jnp.asarray(lengths, jnp.int32))

    lengths = jnp.where(number % 4 == 0, named(packed, number // 4), named(ordinary, number - number // 4 - 1))
    mixed = jax.random.permutation(jax.random.fold_in(own, 3), count)
    giver, sink = mixed[0:count // 2 * 2:2], mixed[1:count // 2 * 2:2]
    margin = jnp.minimum(lengths[giver] - 1, bound - lengths[sink]) // 2
    margin = jnp.where((giver == order[0]) | (sink == order[0]) | (lengths[sink] == 0), 0, jnp.maximum(margin, 0))
    passed = jax.random.randint(jax.random.fold_in(own, 4), (count // 2,), 0, 1 << 20) % (margin + 1)
    lengths = lengths.at[giver].add(-passed).at[sink].add(passed)
    members = jnp.searchsorted(jnp.cumsum(lengths), jnp.arange(rows * top), side="right").astype(jnp.int32)
    table = members.reshape(top, rows).T
    table = table[jax.random.permutation(jax.random.fold_in(own, 1), rows)]
    turn = jax.random.randint(jax.random.fold_in(own, 2), (rows, 1), 0, top)
    return jnp.take_along_axis(table, (jnp.arange(top)[None, :] + turn) % top, axis=1)


def portions_of(number_of, total, limit, skew, full):
    loads = [(1 << 20) // math.isqrt(rank ** skew) + 1 for rank in range(1, number_of + 1)]
    largest = limit if full else min(limit, max(-(-total // number_of), total * loads[0] // sum(loads)))
    least = 1 if total - largest >= number_of - 1 else 0
    counts, spare = [largest] + [least] * (number_of - 1), total - largest - least * (number_of - 1)
    while spare > 0:
        free = [i for i in range(1, number_of) if counts[i] < largest] or [i for i in range(1, number_of) if counts[i] < limit]
        whole, remaining = sum([loads[i] for i in free]), spare
        for i in free:
            addition = min(limit - counts[i], max(1, remaining * loads[i] // whole), spare)
            counts[i] = counts[i] + addition
            spare = spare - addition
    return np.array(counts)


def noise_with(own_key, extent, width, bound, shards, heavy, held_as=jnp.bfloat16):
    entries = width * jax.random.normal(own_key, extent, jnp.float32)
    if shards:
        entries = entries * steps_of(own_key, extent, shards, -0.22, 0.18)
    return jnp.clip(with_spikes(entries, jax.random.fold_in(own_key, 3), *heavy), -bound, bound).astype(held_as)


def setup_inputs(seed: int = 0) -> dict:
    key_of = jax.random.split(jax.random.key(seed), 6)
    queries = draw_queries(jax.random.fold_in(key_of[5], 71), 0)
    prefix_kv = draw_prefix_kv(jax.random.fold_in(key_of[5], 71), 0)
    suffix_kv = draw_suffix_kv(jax.random.fold_in(key_of[5], 71), 0)
    candidate_prefix_keys = jax.random.split(jax.random.fold_in(key_of[3], 1), CANDS // CAND_DEV)
    candidate_prefix_turns = jax.random.permutation(jax.random.fold_in(key_of[3], 3), CANDS // CAND_DEV)
    candidate_prefix = jax.vmap(lambda own, number: routed_block(jax.random.fold_in(key_of[3], 2), own, number, CAND_DEV, N_CACHE, 1, CAP, 2))(candidate_prefix_keys, candidate_prefix_turns).reshape((CANDS, 1))
    w_out = noise_with(key_of[4], (H * HD, DOUT), (H * HD // 128) ** -0.5, 1.0, ((0, 8),), (0, 1, 8, 2.0))
    return dict(queries=queries, prefix_kv=prefix_kv, suffix_kv=suffix_kv, candidate_prefix=candidate_prefix, w_out=w_out)


def prefix_part(query_rows, key_rows, value_rows):
    row_count = query_rows.shape[0]
    kv_heads = key_rows.shape[1] // HD
    query_heads = query_rows.astype(jnp.float32).reshape(row_count, kv_heads, H // KVH, HD)
    key_heads = key_rows.astype(jnp.float32).reshape(-1, kv_heads, HD)
    value_heads = value_rows.astype(jnp.float32).reshape(-1, kv_heads, HD)
    scores = jnp.einsum('rkgd,lkd->rkgl', query_heads, key_heads) * (1.0 / math.sqrt(HD))
    row_max = lax.optimization_barrier(jnp.max(scores, axis=-1, keepdims=True))
    exp_scores = jnp.exp(scores - row_max)
    row_total = lax.optimization_barrier(jnp.sum(exp_scores, axis=-1, keepdims=True))
    weights = lax.optimization_barrier(exp_scores.astype(jnp.bfloat16)).astype(jnp.float32)
    summed = jnp.einsum('rkgl,lkd->rkgd', weights, value_heads)
    prefix_out = (summed / row_total).astype(jnp.bfloat16)
    return (prefix_out, row_max[..., 0], row_total[..., 0])

def suffix_part(query_rows, key_rows, value_rows):
    batch, length = (query_rows.shape[0], query_rows.shape[1])
    kv_heads = key_rows.shape[2] // HD
    query_heads = query_rows.astype(jnp.float32).reshape(batch, length, kv_heads, H // KVH, HD)
    key_heads = key_rows.astype(jnp.float32).reshape(batch, length, kv_heads, HD)
    value_heads = value_rows.astype(jnp.float32).reshape(batch, length, kv_heads, HD)
    scores = jnp.einsum('btkgd,bukd->btkgu', query_heads, key_heads) * (1.0 / math.sqrt(HD))
    position = jnp.arange(length)
    causal_mask = (position[:, None] >= position[None, :])[None, :, None, None, :]
    row_max = lax.optimization_barrier(jnp.max(jnp.where(causal_mask, scores, -jnp.inf), axis=-1, keepdims=True))
    exp_scores = jnp.where(causal_mask, jnp.exp(scores - row_max), 0.0)
    row_total = lax.optimization_barrier(jnp.sum(exp_scores, axis=-1))
    weights = lax.optimization_barrier(exp_scores.astype(jnp.bfloat16)).astype(jnp.float32)
    summed = jnp.einsum('btkgu,bukd->btkgd', weights, value_heads)
    return (summed, row_max[..., 0], row_total)

def combine_parts(prefix_out, prefix_max, prefix_total, suffix_sum, suffix_max, suffix_total):
    joint_max = jnp.maximum(prefix_max, suffix_max)
    prefix_gain = prefix_total * jnp.exp(prefix_max - joint_max)
    suffix_gain = jnp.exp(suffix_max - joint_max)
    upper = prefix_gain[..., None] * prefix_out.astype(jnp.float32) + suffix_gain[..., None] * suffix_sum
    lower = prefix_gain + suffix_gain * suffix_total
    return (upper / lower[..., None]).astype(jnp.bfloat16)

def reference(queries, prefix_kv, suffix_kv, candidate_prefix, w_out):

    def one_candidate(items):
        query_rows, suffix_keys, suffix_values, prefix_id = items
        key_rows = lax.dynamic_index_in_dim(prefix_kv[0], prefix_id, 0, keepdims=False)
        value_rows = lax.dynamic_index_in_dim(prefix_kv[1], prefix_id, 0, keepdims=False)
        prefix_out, prefix_max, prefix_total = prefix_part(query_rows, key_rows, value_rows)
        suffix_sum, suffix_max, suffix_total = suffix_part(query_rows[None], suffix_keys[None], suffix_values[None])
        attention = combine_parts(prefix_out[None], prefix_max[None], prefix_total[None], suffix_sum, suffix_max, suffix_total)
        return attention.reshape(SUF, H * HD)
    attention = lax.map(one_candidate, (queries, suffix_kv[0], suffix_kv[1], candidate_prefix[:, 0]))
    projected = jnp.dot(attention.reshape(CANDS * SUF, H * HD), w_out, preferred_element_type=jnp.float32)
    return projected.astype(jnp.bfloat16).reshape(CANDS, SUF, DOUT)
```

```python
import functools
import math

import jax
import jax.numpy as jnp
from jax import lax
from jax.experimental import pallas as pl
from jax.experimental.pallas import tpu as pltpu
from jax.sharding import PartitionSpec as P

H = 64
KVH = 8
HD = 128
GROUP = H // KVH
NX = 4
NZ = 8
NY = 4
LOG2E = 1.4426950408889634
MIB = 1024 * 1024


def send_cache(value, step_x, step_z):
    pairs = [
        (x * NZ + z, ((x + step_x) % NX) * NZ + (z + step_z) % NZ)
        for x in range(NX)
        for z in range(NZ)
    ]
    return lax.ppermute(value, "cache", pairs)


def send_y(value, step):
    pairs = [(2 * y + c, 2 * ((y + step) % NY) + c) for y in range(NY) for c in range(2)]
    return lax.ppermute(value, "tensor", pairs)


def swap_core(value):
    return lax.ppermute(value, "tensor", [(t, t ^ 1) for t in range(2 * NY)])


def gather_prefix(block):
    pieces = []

    def whole(array, dz, dx):
        for kv in range(2):
            pieces.append((array, kv, kv, (dz % NZ) * NX + dx % NX, 0))

    def part(array, at, kv, dz, dx, first=0):
        pieces.append((array, at, kv, (dz % NZ) * NX + dx % NX, first))

    whole(block, 0, 0)
    from_z = {}
    from_x = {}
    from_z[1] = send_cache(block, 0, -1)
    from_z[-1] = send_cache(block, 0, 1)
    from_x[1] = send_cache(block, -1, 0)
    from_x[-1] = send_cache(block, 1, 0)
    whole(from_x[1], 0, 1)
    whole(from_x[-1], 0, -1)
    key_x2 = send_cache(from_x[1][0:1], -1, 0)
    value_x2 = send_cache(from_x[-1][1:2], 1, 0)
    part(key_x2, 0, 0, 0, 2)
    part(value_x2, 0, 1, 0, 2)
    for step in (2, 3):
        from_z[step] = send_cache(from_z[step - 1], 0, -1)
        from_z[-step] = send_cache(from_z[1 - step], 0, 1)
    for step in (1, 2, 3):
        whole(from_z[step], step, 0)
        whole(from_z[-step], -step, 0)
    key_z4 = send_cache(from_z[3][0:1], 0, -1)
    value_z4 = send_cache(from_z[-3][1:2], 0, 1)
    part(key_z4, 0, 0, 4, 0)
    part(value_z4, 0, 1, 4, 0)

    values = jnp.concatenate([from_x[1][1:2], from_x[-1][1:2], value_x2], axis=0)
    dxs = (1, -1, 2)
    ahead, behind = values, values
    for step in (1, 2, 3):
        ahead = send_cache(ahead, 0, -1)
        behind = send_cache(behind, 0, 1)
        for at, dx in enumerate(dxs):
            part(ahead, at, 1, step, dx)
            part(behind, at, 1, -step, dx)
    length = block.shape[1]
    half = length // 2
    upper = send_cache(ahead[:, :half], 0, -1)
    lower = send_cache(behind[:, half:], 0, 1)
    for at, dx in enumerate(dxs):
        part(upper, at, 1, 4, dx, 0)
        part(lower, at, 1, 4, dx, half)

    near = jnp.concatenate(
        [from_z[1][0:1], from_z[-1][0:1], from_z[2][0:1], from_z[-2][0:1]], axis=0
    )
    ahead, behind = send_cache(near, -1, 0), send_cache(near, 1, 0)
    far_a, far_b = send_cache(ahead[:2], -1, 0), send_cache(behind[2:], 1, 0)
    for at, dz in enumerate((1, -1, 2, -2)):
        part(ahead, at, 0, dz, 1)
        part(behind, at, 0, dz, -1)
        part(far_a if at < 2 else far_b, at % 2, 0, dz, 2)
    distant = jnp.concatenate([from_z[3][0:1], from_z[-3][0:1], key_z4], axis=0)
    ahead, behind = send_cache(distant, -1, 0), send_cache(distant, 1, 0)
    upper, lower = send_cache(ahead[:, :half], -1, 0), send_cache(behind[:, half:], 1, 0)
    for at, dz in enumerate((3, -3, 4)):
        part(ahead, at, 0, dz, 1)
        part(behind, at, 0, dz, -1)
        part(upper, at, 0, dz, 2, 0)
        part(lower, at, 0, dz, 2, half)
    return pieces


def attention_kernel(places, n_arrays, per_step, codes, q_ref, s_ref, *rest):
    arrays = rest[:n_arrays]
    o_ref, cache, sems = rest[n_arrays:]
    step = pl.program_id(0)

    def copies():
        for n, (which, at, kv, code, first) in enumerate(places):
            rows = arrays[which].shape[1]
            yield pltpu.make_async_copy(
                arrays[which].at[at],
                cache.at[kv, code, pl.ds(first, rows)],
                sems.at[n],
            )

    @pl.when(step == 0)
    def _():
        for copy in copies():
            copy.start()
        for copy in copies():
            copy.wait()

    suffix = q_ref.shape[1]
    rows = GROUP * suffix
    factor = LOG2E / math.sqrt(HD)
    token = lax.broadcasted_iota(jnp.int32, (rows, suffix), 0) % suffix
    other = lax.broadcasted_iota(jnp.int32, (rows, suffix), 1)
    causal = other <= token
    contract_last = (((1,), (1,)), ((), ()))
    contract = (((1,), (0,)), ((), ()))
    for i in range(per_step):
        code = codes[step * per_step + i]
        q = jnp.concatenate([q_ref[i, :, g * HD : (g + 1) * HD] for g in range(GROUP)], axis=0)
        far = lax.dot_general(q, cache[0, code], contract_last, preferred_element_type=jnp.float32)
        near = lax.dot_general(q, s_ref[0, i], contract_last, preferred_element_type=jnp.float32)
        near = jnp.where(causal, near, -jnp.inf)
        top = jnp.maximum(
            jnp.max(far, axis=1, keepdims=True), jnp.max(near, axis=1, keepdims=True)
        )
        far = jnp.exp2((far - top) * factor)
        near = jnp.exp2((near - top) * factor)
        total = jnp.sum(far, axis=1, keepdims=True) + jnp.sum(near, axis=1, keepdims=True)
        summed = lax.dot_general(
            far.astype(jnp.bfloat16), cache[1, code], contract, preferred_element_type=jnp.float32
        ) + lax.dot_general(
            near.astype(jnp.bfloat16), s_ref[1, i], contract, preferred_element_type=jnp.float32
        )
        out = (summed / total).astype(jnp.bfloat16)
        for g in range(GROUP):
            o_ref[i, :, g * HD : (g + 1) * HD] = out[g * suffix : (g + 1) * suffix]


def attend(codes, queries, suffix_kv, pieces, length):
    arrays = []
    places = []
    for array, at, kv, code, first in pieces:
        which = next((n for n, a in enumerate(arrays) if a is array), len(arrays))
        if which == len(arrays):
            arrays.append(array)
        places.append((which, at, kv, code, first))
    count, suffix, width = queries.shape
    per_step = 2
    return pl.pallas_call(
        functools.partial(attention_kernel, places, len(arrays), per_step),
        out_shape=jax.ShapeDtypeStruct(queries.shape, jnp.bfloat16),
        grid_spec=pltpu.PrefetchScalarGridSpec(
            num_scalar_prefetch=1,
            grid=(count // per_step,),
            in_specs=[
                pl.BlockSpec((per_step, suffix, width), lambda n, c: (n, 0, 0)),
                pl.BlockSpec((2, per_step, suffix, HD), lambda n, c: (0, n, 0, 0)),
            ]
            + [pl.BlockSpec(memory_space=pl.ANY)] * len(arrays),
            out_specs=pl.BlockSpec((per_step, suffix, width), lambda n, c: (n, 0, 0)),
            scratch_shapes=[
                pltpu.VMEM((2, NX * NZ, length, HD), jnp.bfloat16),
                pltpu.SemaphoreType.DMA((len(places),)),
            ],
        ),
        compiler_params=pltpu.CompilerParams(vmem_limit_bytes=24 * MIB),
        cost_estimate=pl.CostEstimate(
            flops=4 * count * suffix * width * length,
            bytes_accessed=16 * MIB,
            transcendentals=count * suffix * GROUP * length,
        ),
    )(codes, queries, suffix_kv, *arrays)


def pick_kernel(place, w_ref, o_ref):
    o_ref[0] = w_ref[...]


def pick_columns(place, w_out, width):
    depth = w_out.shape[0]
    return pl.pallas_call(
        pick_kernel,
        out_shape=jax.ShapeDtypeStruct((NY, depth, width), w_out.dtype),
        grid_spec=pltpu.PrefetchScalarGridSpec(
            num_scalar_prefetch=1,
            grid=(NY,),
            in_specs=[pl.BlockSpec((depth, width), lambda n, p: (0, 2 * n + 1 - p[1]))],
            out_specs=pl.BlockSpec((1, depth, width), lambda n, p: (n, 0, 0)),
        ),
        compiler_params=pltpu.CompilerParams(vmem_limit_bytes=8 * MIB),
        cost_estimate=pl.CostEstimate(flops=0, bytes_accessed=8 * MIB, transcendentals=0),
    )(place, w_out)


def project_kernel(place, a_ref, b_ref, wa_ref, wb_ref, o_ref):
    total = jnp.dot(a_ref[...], wa_ref[...], preferred_element_type=jnp.float32)
    total += jnp.dot(b_ref[...], wb_ref[0], preferred_element_type=jnp.float32)
    o_ref[...] = total.astype(jnp.bfloat16)


def project(place, mine, mate, w_out, w_mate, turn, first, rows):
    depth, width = w_mate.shape[1:]
    tile = min(256, rows)
    base = first // tile

    def column(n, p):
        return (0, 2 * ((p[0] + turn) % NY) + p[1])

    def block(n, p):
        return ((p[0] + turn) % NY, 0, 0)

    return pl.pallas_call(
        project_kernel,
        out_shape=jax.ShapeDtypeStruct((rows, width), jnp.bfloat16),
        grid_spec=pltpu.PrefetchScalarGridSpec(
            num_scalar_prefetch=1,
            grid=(rows // tile,),
            in_specs=[
                pl.BlockSpec((tile, depth), lambda n, p: (base + n, 0)),
                pl.BlockSpec((tile, depth), lambda n, p: (base + n, 0)),
                pl.BlockSpec((depth, width), column),
                pl.BlockSpec((1, depth, width), block),
            ],
            out_specs=pl.BlockSpec((tile, width), lambda n, p: (n, 0)),
        ),
        compiler_params=pltpu.CompilerParams(vmem_limit_bytes=16 * MIB),
        cost_estimate=pl.CostEstimate(
            flops=4 * rows * depth * width, bytes_accessed=6 * MIB, transcendentals=0
        ),
    )(place, mine, mate, w_out, w_mate)


def added(*terms):
    return sum(t.astype(jnp.float32) for t in terms).astype(jnp.bfloat16)


def shards(queries, prefix_kv, suffix_kv, candidate_prefix, w_out):
    count, suffix, width = queries.shape
    length = prefix_kv.shape[2]
    out_width = w_out.shape[1] // (2 * NY)
    me = lax.axis_index("cache")
    t = lax.axis_index("tensor")
    place = jnp.stack([t // 2, t % 2]).astype(jnp.int32)
    ids = candidate_prefix[:, 0]
    codes = ((ids % NZ - me % NZ) % NZ) * NX + (ids // NZ - me // NZ) % NX

    pieces = gather_prefix(prefix_kv.reshape(2, length, HD))
    w_mate = swap_core(pick_columns(place, w_out, out_width))
    mine = attend(codes, queries, suffix_kv, pieces, length).reshape(count * suffix, width)
    mate = swap_core(mine)

    rows = count * suffix
    half = rows // 2
    part = functools.partial(project, place, mine, mate, w_out, w_mate)
    top2 = send_y(part(2, 0, half), 1)
    low2 = send_y(part(2, half, half), -1)
    low1 = send_y(part(1, half, half), 1)
    top3 = send_y(part(3, 0, half), -1)
    own_top1 = part(1, 0, half)
    own_low3 = part(3, half, half)
    top1 = send_y(added(own_top1, top2), 1)
    low3 = send_y(added(own_low3, low2), -1)
    own_top = part(0, 0, half)
    own_low = part(0, half, half)
    top = added(own_top, top1, top3)
    low = added(own_low, low1, low3)
    return jnp.concatenate([top, low], axis=0).reshape(count, suffix, out_width)


def solution(mesh):
    in_specs = (
        P("cache", None, "tensor"),
        P(None, "cache", None, "tensor"),
        P(None, "cache", None, "tensor"),
        P("cache", None),
        P("tensor", None),
    )
    out_specs = P("cache", None, "tensor")
    return jax.shard_map(shards, mesh=mesh, in_specs=in_specs, out_specs=out_specs, check_vma=False)
```

```python
import functools
import math

import jax
import jax.numpy as jnp
from jax import lax
from jax.experimental import pallas as pl
from jax.experimental.pallas import tpu as pltpu
from jax.sharding import PartitionSpec as P

H = 64
KVH = 8
HD = 128
GROUP = H // KVH
NX = 4
NZ = 8
NY = 4
LOG2E = 1.4426950408889634
MIB = 1024 * 1024


def send_cache(value, step_x, step_z):
    pairs = [
        (x * NZ + z, ((x + step_x) % NX) * NZ + (z + step_z) % NZ)
        for x in range(NX)
        for z in range(NZ)
    ]
    return lax.ppermute(value, "cache", pairs)


def send_y(value, step):
    pairs = [(2 * y + c, 2 * ((y + step) % NY) + c) for y in range(NY) for c in range(2)]
    return lax.ppermute(value, "tensor", pairs)


def swap_core(value):
    return lax.ppermute(value, "tensor", [(t, t ^ 1) for t in range(2 * NY)])


def together(*values):
    return lax.optimization_barrier(values)


def gather_prefix(block):
    pieces = []
    length = block.shape[1]
    half = length // 2

    def whole(array, dz, dx):
        for kv in range(2):
            part(array, kv, kv, dz, dx)

    def part(array, at, kv, dz, dx, first=0):
        pieces.append((array, at, kv, (dz % NZ) * NX + dx % NX, first))

    whole(block, 0, 0)
    z1a, z1b = send_cache(block, 0, -1), send_cache(block, 0, 1)
    x1a, x1b = send_cache(block, -1, 0), send_cache(block, 1, 0)
    z1a, z1b, x1a, x1b = together(z1a, z1b, x1a, x1b)
    z2a, z2b = send_cache(z1a, 0, -1), send_cache(z1b, 0, 1)
    key_x2, value_x2 = send_cache(x1a[0:1], -1, 0), send_cache(x1b[1:2], 1, 0)
    z2a, z2b, key_x2, value_x2 = together(z2a, z2b, key_x2, value_x2)
    z3a, z3b = send_cache(z2a, 0, -1), send_cache(z2b, 0, 1)
    near = jnp.concatenate([z1a[0:1], z1b[0:1], z2a[0:1], z2b[0:1]], axis=0)
    near_a, near_b = send_cache(near, -1, 0), send_cache(near, 1, 0)
    values = jnp.concatenate([x1a[1:2], x1b[1:2], value_x2], axis=0)
    v1a, v1b = send_cache(values, 0, -1), send_cache(values, 0, 1)
    z3a, z3b, near_a, near_b, v1a, v1b = together(z3a, z3b, near_a, near_b, v1a, v1b)
    key_z4, value_z4 = send_cache(z3a[0:1], 0, -1), send_cache(z3b[1:2], 0, 1)
    near_c, near_d = send_cache(near_a[:2], -1, 0), send_cache(near_b[2:], 1, 0)
    v2a, v2b = send_cache(v1a, 0, -1), send_cache(v1b, 0, 1)
    key_z4, value_z4, near_c, near_d, v2a, v2b = together(
        key_z4, value_z4, near_c, near_d, v2a, v2b
    )
    v3a, v3b = send_cache(v2a, 0, -1), send_cache(v2b, 0, 1)
    distant = jnp.concatenate([z3a[0:1], z3b[0:1], key_z4], axis=0)
    far_a, far_b = send_cache(distant, -1, 0), send_cache(distant, 1, 0)
    v3a, v3b, far_a, far_b = together(v3a, v3b, far_a, far_b)
    v4a, v4b = send_cache(v3a[:, :half], 0, -1), send_cache(v3b[:, half:], 0, 1)
    far_c, far_d = send_cache(far_a[:, :half], -1, 0), send_cache(far_b[:, half:], 1, 0)

    for step, ahead, behind in ((1, z1a, z1b), (2, z2a, z2b), (3, z3a, z3b)):
        whole(ahead, step, 0)
        whole(behind, -step, 0)
    part(key_z4, 0, 0, 4, 0)
    part(value_z4, 0, 1, 4, 0)
    whole(x1a, 0, 1)
    whole(x1b, 0, -1)
    part(key_x2, 0, 0, 0, 2)
    part(value_x2, 0, 1, 0, 2)
    for at, dx in enumerate((1, -1, 2)):
        for step, ahead, behind in ((1, v1a, v1b), (2, v2a, v2b), (3, v3a, v3b)):
            part(ahead, at, 1, step, dx)
            part(behind, at, 1, -step, dx)
        part(v4a, at, 1, 4, dx, 0)
        part(v4b, at, 1, 4, dx, half)
    for at, dz in enumerate((1, -1, 2, -2)):
        part(near_a, at, 0, dz, 1)
        part(near_b, at, 0, dz, -1)
        part(near_c if at < 2 else near_d, at % 2, 0, dz, 2)
    for at, dz in enumerate((3, -3, 4)):
        part(far_a, at, 0, dz, 1)
        part(far_b, at, 0, dz, -1)
        part(far_c, at, 0, dz, 2, 0)
        part(far_d, at, 0, dz, 2, half)
    return pieces


LAST = (((1,), (1,)), ((), ()))
INNER = (((1,), (0,)), ((), ()))


def beside_ones(values):
    return jnp.concatenate([values, jnp.ones_like(values)], axis=1)


def attention_kernel(places, n_arrays, batch, codes, q_ref, s_ref, *rest):
    arrays = rest[:n_arrays]
    o_ref, cache, sems = rest[n_arrays:]
    count, suffix, _ = q_ref.shape
    rows = GROUP * suffix
    factor = LOG2E / math.sqrt(HD)

    def copies():
        for n, (which, at, kv, code, first) in enumerate(places):
            yield pltpu.make_async_copy(
                arrays[which].at[at],
                cache.at[kv, code, pl.ds(first, arrays[which].shape[1])],
                sems.at[n],
            )

    for copy in copies():
        copy.start()
    for copy in copies():
        copy.wait()

    token = lax.broadcasted_iota(jnp.int32, (rows, HD), 0) % suffix
    causal = lax.broadcasted_iota(jnp.int32, (rows, HD), 1) <= token
    blank = jnp.zeros((HD - suffix, HD), jnp.bfloat16)

    @pl.loop(0, count // batch)
    def _(step):
        scores = []
        for i in range(batch):
            n = step * batch + i
            q = jnp.concatenate([q_ref[n, :, g * HD : (g + 1) * HD] for g in range(GROUP)], axis=0)
            far = lax.dot_general(
                q, cache[0, codes[n]], LAST, preferred_element_type=jnp.float32
            )
            keys = jnp.concatenate([s_ref[0, n], blank], axis=0)
            near = lax.dot_general(q, keys, LAST, preferred_element_type=jnp.float32)
            near = jnp.where(causal, near, -jnp.inf)
            tiles = [far[:, j : j + HD] for j in range(0, far.shape[1], HD)]
            scores.append(tiles + [near])
        weights = []
        for tiles in scores:
            top = jnp.max(functools.reduce(jnp.maximum, tiles), axis=1, keepdims=True)
            weights.append([jnp.exp2((s - top) * factor).astype(jnp.bfloat16) for s in tiles])
        for i in range(batch):
            n = step * batch + i
            far = jnp.concatenate(weights[i][:-1], axis=1)
            near = weights[i][-1][:, :suffix]
            summed = lax.dot_general(
                far, beside_ones(cache[1, codes[n]]), INNER, preferred_element_type=jnp.float32
            ) + lax.dot_general(
                near, beside_ones(s_ref[1, n]), INNER, preferred_element_type=jnp.float32
            )
            out = (summed[:, :HD] / summed[:, HD:]).astype(jnp.bfloat16)
            for g in range(GROUP):
                o_ref[n, :, g * HD : (g + 1) * HD] = out[g * suffix : (g + 1) * suffix]


def attend(codes, queries, suffix_kv, pieces, length):
    arrays = []
    places = []
    for array, at, kv, code, first in pieces:
        which = next((n for n, a in enumerate(arrays) if a is array), len(arrays))
        if which == len(arrays):
            arrays.append(array)
        places.append((which, at, kv, code, first))
    count, suffix, width = queries.shape
    vmem = pl.BlockSpec(memory_space=pltpu.VMEM)
    return pl.pallas_call(
        functools.partial(attention_kernel, places, len(arrays), 4),
        out_shape=jax.ShapeDtypeStruct(queries.shape, jnp.bfloat16),
        in_specs=[pl.BlockSpec(memory_space=pltpu.SMEM), vmem, vmem]
        + [pl.BlockSpec(memory_space=pl.ANY)] * len(arrays),
        out_specs=vmem,
        scratch_shapes=[
            pltpu.VMEM((2, NX * NZ, length, HD), jnp.bfloat16),
            pltpu.SemaphoreType.DMA((len(places),)),
        ],
        compiler_params=pltpu.CompilerParams(vmem_limit_bytes=24 * MIB),
        cost_estimate=pl.CostEstimate(
            flops=4 * count * suffix * width * length,
            bytes_accessed=16 * MIB,
            transcendentals=count * suffix * GROUP * length,
        ),
    )(codes, queries, suffix_kv, *arrays)


def pick_kernel(place, w_ref, o_ref, sems):
    width = o_ref.shape[2]
    copies = [
        pltpu.make_async_copy(
            w_ref.at[:, pl.ds(pl.multiple_of((2 * n + 1 - place[1]) * width, width), width)],
            o_ref.at[n],
            sems.at[n],
        )
        for n in range(NY)
    ]
    for copy in copies:
        copy.start()
    for copy in copies:
        copy.wait()


def pick_columns(place, w_out, width):
    hbm = pl.BlockSpec(memory_space=pltpu.HBM)
    return pl.pallas_call(
        pick_kernel,
        out_shape=jax.ShapeDtypeStruct((NY, w_out.shape[0], width), w_out.dtype),
        in_specs=[pl.BlockSpec(memory_space=pltpu.SMEM), hbm],
        out_specs=hbm,
        scratch_shapes=[pltpu.SemaphoreType.DMA((NY,))],
        cost_estimate=pl.CostEstimate(flops=0, bytes_accessed=8 * MIB, transcendentals=0),
    )(place, w_out)


def project_kernel(tiles, place, a_ref, b_ref, w_ref, m_ref, *outs):
    total = jnp.dot(a_ref[...], w_ref[...], preferred_element_type=jnp.float32)
    total += jnp.dot(b_ref[...], m_ref[0], preferred_element_type=jnp.float32)
    total = total.astype(jnp.bfloat16)
    for at, out in enumerate(outs):

        @pl.when(pl.program_id(0) // tiles == at)
        def _(out=out):
            out[...] = total


def project(place, mine, mate, w_out, w_mate, parts, rows):
    depth, width = w_mate.shape[1:]
    tile = min(256, rows)
    tiles = rows // tile

    def pick(n, choices):
        value = choices[-1]
        for at in range(len(choices) - 2, -1, -1):
            value = jnp.where(n // tiles == at, choices[at], value)
        return value

    def row(n, p):
        return (pick(n, [first // tile for _, first in parts]) + n % tiles, 0)

    def chip(n, p):
        return (p[0] + pick(n, [turn for turn, _ in parts])) % NY

    def out(at):
        return lambda n, p: (jnp.clip(n - at * tiles, 0, tiles - 1), 0)

    hbm = pltpu.HBM
    return pl.pallas_call(
        functools.partial(project_kernel, tiles),
        out_shape=[jax.ShapeDtypeStruct((rows, width), jnp.bfloat16)] * len(parts),
        grid_spec=pltpu.PrefetchScalarGridSpec(
            num_scalar_prefetch=1,
            grid=(tiles * len(parts),),
            in_specs=[
                pl.BlockSpec((tile, depth), row),
                pl.BlockSpec((tile, depth), row),
                pl.BlockSpec((depth, width), lambda n, p: (0, 2 * chip(n, p) + p[1])),
                pl.BlockSpec((1, depth, width), lambda n, p: (chip(n, p), 0, 0)),
            ],
            out_specs=[pl.BlockSpec((tile, width), out(at)) for at in range(len(parts))],
        ),
        compiler_params=pltpu.CompilerParams(vmem_limit_bytes=24 * MIB),
        cost_estimate=pl.CostEstimate(
            flops=4 * rows * len(parts) * depth * width,
            bytes_accessed=6 * MIB,
            transcendentals=0,
        ),
    )(place, mine, mate, w_out, w_mate)


def final_kernel(own, top1, top3, low1, low3, o_ref):
    half = top1.shape[0]
    for first, a, b in ((0, top1, top3), (half, low1, low3)):
        total = own[first : first + half].astype(jnp.float32) + a[...] + b[...]
        o_ref[first : first + half] = total.astype(jnp.bfloat16)


def added(*terms):
    return sum(t.astype(jnp.float32) for t in terms).astype(jnp.bfloat16)


def shards(queries, prefix_kv, suffix_kv, candidate_prefix, w_out):
    count, suffix, width = queries.shape
    length = prefix_kv.shape[2]
    out_width = w_out.shape[1] // (2 * NY)
    me = lax.axis_index("cache")
    t = lax.axis_index("tensor")
    place = jnp.stack([t // 2, t % 2]).astype(jnp.int32)
    ids = candidate_prefix[:, 0]
    codes = ((ids % NZ - me % NZ) % NZ) * NX + (ids // NZ - me // NZ) % NX

    pieces = gather_prefix(prefix_kv.reshape(2, length, HD))
    w_mate = swap_core(pick_columns(place, w_out, out_width))
    mine = attend(codes, queries, suffix_kv, pieces, length).reshape(count * suffix, width)
    mate = swap_core(mine)

    rows = count * suffix
    half = rows // 2
    part = functools.partial(project, place, mine, mate, w_out, w_mate)
    top2, low2 = part([(2, 0), (2, half)], half)
    top2, low2 = send_y(top2, 1), send_y(low2, -1)
    low1, top3 = part([(1, half), (3, 0)], half)
    low1, top3 = send_y(low1, 1), send_y(top3, -1)
    own_top1, own_low3 = part([(1, 0), (3, half)], half)
    top1 = send_y(added(own_top1, top2), 1)
    low3 = send_y(added(own_low3, low2), -1)
    (own,) = part([(0, 0)], rows)
    vmem = pl.BlockSpec(memory_space=pltpu.VMEM)
    out = pl.pallas_call(
        final_kernel,
        out_shape=jax.ShapeDtypeStruct((rows, out_width), jnp.bfloat16),
        in_specs=[vmem] * 5,
        out_specs=vmem,
        compiler_params=pltpu.CompilerParams(vmem_limit_bytes=16 * MIB),
    )(own, top1, top3, low1, low3)
    return out.reshape(count, suffix, out_width)


def solution(mesh):
    in_specs = (
        P("cache", None, "tensor"),
        P(None, "cache", None, "tensor"),
        P(None, "cache", None, "tensor"),
        P("cache", None),
        P("tensor", None),
    )
    out_specs = P("cache", None, "tensor")
    return jax.shard_map(shards, mesh=mesh, in_specs=in_specs, out_specs=out_specs, check_vma=False)
```

```python
import functools
import math

import jax
import jax.numpy as jnp
from jax import lax
from jax.experimental import pallas as pl
from jax.experimental.pallas import tpu as pltpu
from jax.sharding import PartitionSpec as P

H = 64
KVH = 8
HD = 128
GROUP = H // KVH
NX = 4
NZ = 8
NY = 4
LOG2E = 1.4426950408889634
MIB = 1024 * 1024


def send_cache(value, step_x, step_z):
    pairs = [
        (x * NZ + z, ((x + step_x) % NX) * NZ + (z + step_z) % NZ)
        for x in range(NX)
        for z in range(NZ)
    ]
    return lax.ppermute(value, "cache", pairs)


def send_y(value, step):
    pairs = [(2 * y + c, 2 * ((y + step) % NY) + c) for y in range(NY) for c in range(2)]
    return lax.ppermute(value, "tensor", pairs)


def swap_core(value):
    return lax.ppermute(value, "tensor", [(t, t ^ 1) for t in range(2 * NY)])


def together(*values):
    return lax.optimization_barrier(values)


class Gather:
    def __init__(self, block):
        self.block = block
        self.half = block.shape[1] // 2
        self.sources = {}

    def part(self, array, at, kv, dz, dx, first=0):
        code = (dz % NZ) * NX + dx % NX
        self.sources.setdefault(code, []).append((array, at, kv, first))

    def whole(self, array, dz, dx):
        for kv in range(2):
            self.part(array, kv, kv, dz, dx)

    def early(self):
        block = self.block
        z1a, z1b = send_cache(block, 0, -1), send_cache(block, 0, 1)
        x1a, x1b = send_cache(block, -1, 0), send_cache(block, 1, 0)
        z2a, z2b = send_cache(z1a, 0, -1), send_cache(z1b, 0, 1)
        key_x2, value_x2 = send_cache(x1a[0:1], -1, 0), send_cache(x1b[1:2], 1, 0)
        values = jnp.concatenate([x1a[1:2], x1b[1:2], value_x2], axis=0)
        near = jnp.concatenate([z1a[0:1], z1b[0:1], z2a[0:1], z2b[0:1]], axis=0)
        near_a, near_b = send_cache(near, -1, 0), send_cache(near, 1, 0)
        z3a, z3b = send_cache(z2a, 0, -1), send_cache(z2b, 0, 1)
        v1a, v1b = send_cache(values, 0, -1), send_cache(values, 0, 1)
        v1a, v1b, near_a, near_b, z3a, z3b = together(v1a, v1b, near_a, near_b, z3a, z3b)
        key_z4, value_z4 = send_cache(z3a[0:1], 0, -1), send_cache(z3b[1:2], 0, 1)
        near_c, near_d = send_cache(near_a[:2], -1, 0), send_cache(near_b[2:], 1, 0)
        v2a, v2b = send_cache(v1a, 0, -1), send_cache(v1b, 0, 1)
        v2a, v2b, near_c, near_d, key_z4, value_z4 = together(
            v2a, v2b, near_c, near_d, key_z4, value_z4
        )
        self.whole(block, 0, 0)
        for step, ahead, behind in ((1, z1a, z1b), (2, z2a, z2b), (3, z3a, z3b)):
            self.whole(ahead, step, 0)
            self.whole(behind, -step, 0)
        self.part(key_z4, 0, 0, 4, 0)
        self.part(value_z4, 0, 1, 4, 0)
        self.whole(x1a, 0, 1)
        self.whole(x1b, 0, -1)
        self.part(key_x2, 0, 0, 0, 2)
        self.part(value_x2, 0, 1, 0, 2)
        for at, dx in enumerate((1, -1, 2)):
            for step, ahead, behind in ((1, v1a, v1b), (2, v2a, v2b)):
                self.part(ahead, at, 1, step, dx)
                self.part(behind, at, 1, -step, dx)
        for at, dz in enumerate((1, -1, 2, -2)):
            self.part(near_a, at, 0, dz, 1)
            self.part(near_b, at, 0, dz, -1)
            self.part(near_c if at < 2 else near_d, at % 2, 0, dz, 2)
        self.distant = [z3a[0:1], z3b[0:1], key_z4]
        self.values = v2a, v2b
        return {code: list(parts) for code, parts in self.sources.items()}

    def late(self):
        v2a, v2b = self.values
        distant = jnp.concatenate(self.distant, axis=0)
        v3a, v3b = send_cache(v2a, 0, -1), send_cache(v2b, 0, 1)
        far_a, far_b = send_cache(distant, -1, 0), send_cache(distant, 1, 0)
        self.hop = v3a, v3b, far_a, far_b

    def last(self, token):
        token, v3a, v3b, far_a, far_b = together(token, *self.hop)
        half = self.half
        v4a, v4b = send_cache(v3a[:, :half], 0, -1), send_cache(v3b[:, half:], 0, 1)
        far_c, far_d = send_cache(far_a[:, :half], -1, 0), send_cache(far_b[:, half:], 1, 0)
        for at, dx in enumerate((1, -1, 2)):
            self.part(v3a, at, 1, 3, dx)
            self.part(v3b, at, 1, -3, dx)
            self.part(v4a, at, 1, 4, dx, 0)
            self.part(v4b, at, 1, 4, dx, half)
        for at, dz in enumerate((3, -3, 4)):
            self.part(far_a, at, 0, dz, 1)
            self.part(far_b, at, 0, dz, -1)
            self.part(far_c, at, 0, dz, 2, 0)
            self.part(far_d, at, 0, dz, 2, half)
        return token, self.sources


LAST = (((1,), (1,)), ((), ()))
INNER = (((1,), (0,)), ((), ()))


def beside_ones(values):
    return jnp.concatenate([values, jnp.ones_like(values)], axis=1)


def attention_kernel(sources, n_arrays, lo, batch, order, codes, early, q_ref, s_ref, *rest):
    arrays = rest[:n_arrays]
    *outs, cache, sems = rest[n_arrays:]
    count = cache.shape[0]
    suffix = q_ref.shape[1]
    rows = GROUP * suffix
    factor = LOG2E / math.sqrt(HD)
    token = lax.broadcasted_iota(jnp.int32, (rows, HD), 0) % suffix
    causal = lax.broadcasted_iota(jnp.int32, (rows, HD), 1) <= token
    blank = jnp.zeros((HD - suffix, HD), jnp.bfloat16)

    def fetch(first):
        @pl.loop(0, count)
        def _(i):
            code = codes[order[first + i]]
            for dx in range(NX):

                @pl.when(code % NX == dx)
                def _(dx=dx):
                    for dz in range(NZ):
                        parts = sources.get(dz * NX + dx)
                        if parts is None:
                            continue

                        @pl.when(code // NX == dz)
                        def _(parts=parts):
                            for which, at, kv, row in parts:
                                pltpu.make_async_copy(
                                    arrays[which].at[at],
                                    cache.at[i, kv, pl.ds(row, arrays[which].shape[1])],
                                    sems.at[i],
                                ).start()

    def await_slot(first, i):
        def wait():
            pltpu.make_async_copy(cache.at[i], cache.at[i], sems.at[i]).wait()

        if len(sources) == NX * NZ:
            wait()
        else:
            pl.when(first + i < early[0])(wait)

    def attend_batch(first, step, out):
        scores = []
        for i in range(batch):
            await_slot(first, step * batch + i)
        for i in range(batch):
            n = order[first + step * batch + i]
            q = jnp.concatenate([q_ref[n, :, g * HD : (g + 1) * HD] for g in range(GROUP)], axis=0)
            far = lax.dot_general(
                q, cache[step * batch + i, 0], LAST, preferred_element_type=jnp.float32
            )
            keys = jnp.concatenate([s_ref[0, n], blank], axis=0)
            near = lax.dot_general(q, keys, LAST, preferred_element_type=jnp.float32)
            near = jnp.where(causal, near, -jnp.inf)
            scores.append([far[:, j : j + HD] for j in range(0, far.shape[1], HD)] + [near])
        weights = []
        for tiles in scores:
            top = jnp.max(functools.reduce(jnp.maximum, tiles), axis=1, keepdims=True)
            weights.append([jnp.exp2((s - top) * factor).astype(jnp.bfloat16) for s in tiles])
        for i in range(batch):
            n = order[first + step * batch + i]
            far = jnp.concatenate(weights[i][:-1], axis=1)
            near = weights[i][-1][:, :suffix]
            summed = lax.dot_general(
                far,
                beside_ones(cache[step * batch + i, 1]),
                INNER,
                preferred_element_type=jnp.float32,
            ) + lax.dot_general(
                near, beside_ones(s_ref[1, n]), INNER, preferred_element_type=jnp.float32
            )
            result = (summed[:, :HD] / summed[:, HD:]).astype(jnp.bfloat16)
            for g in range(GROUP):
                out[step * batch + i, :, g * HD : (g + 1) * HD] = result[
                    g * suffix : (g + 1) * suffix
                ]

    def attend_all(first, out):
        fetch(first)

        @pl.loop(0, count // batch)
        def _(step):
            attend_batch(first, step, out)

    attend_all(lo, outs[0])
    if len(outs) > 1:
        @pl.when(early[0] < lo)
        def _():
            attend_all(0, outs[1])


def attend(order, codes, early, queries, suffix_kv, sources, lo, count, length, again):
    arrays = []
    places = {}
    for code, parts in sources.items():
        for array, at, kv, first in parts:
            which = next((n for n, a in enumerate(arrays) if a is array), len(arrays))
            if which == len(arrays):
                arrays.append(array)
            places.setdefault(code, []).append((which, at, kv, first))
    _, suffix, width = queries.shape
    vmem = pl.BlockSpec(memory_space=pltpu.VMEM)
    smem = pl.BlockSpec(memory_space=pltpu.SMEM)
    shape = jax.ShapeDtypeStruct((count, suffix, width), jnp.bfloat16)
    outs = 2 if again else 1
    return pl.pallas_call(
        functools.partial(attention_kernel, places, len(arrays), lo, 4),
        out_shape=[shape] * outs,
        in_specs=[smem] * 3 + [vmem] * 2 + [pl.BlockSpec(memory_space=pl.ANY)] * len(arrays),
        out_specs=[vmem] * outs,
        scratch_shapes=[
            pltpu.VMEM((count, 2, length, HD), jnp.bfloat16),
            pltpu.SemaphoreType.DMA((count,)),
        ],
        compiler_params=pltpu.CompilerParams(vmem_limit_bytes=16 * MIB),
        cost_estimate=pl.CostEstimate(
            flops=4 * count * suffix * width * length,
            bytes_accessed=8 * MIB,
            transcendentals=count * suffix * GROUP * length,
        ),
    )(order, codes, early, queries, suffix_kv, *arrays)


def pick_kernel(place, w_ref, o_ref):
    o_ref[0] = w_ref[...]


def pick_columns(place, w_out, width):
    depth = w_out.shape[0]
    return pl.pallas_call(
        pick_kernel,
        out_shape=jax.ShapeDtypeStruct((NY, depth, width), w_out.dtype),
        grid_spec=pltpu.PrefetchScalarGridSpec(
            num_scalar_prefetch=1,
            grid=(NY,),
            in_specs=[pl.BlockSpec((depth, width), lambda n, p: (0, 2 * n + 1 - p[1]))],
            out_specs=pl.BlockSpec((1, depth, width), lambda n, p: (n, 0, 0)),
        ),
        compiler_params=pltpu.CompilerParams(vmem_limit_bytes=8 * MIB),
        cost_estimate=pl.CostEstimate(flops=0, bytes_accessed=8 * MIB, transcendentals=0),
    )(place, w_out)


def project_kernel(parts, rows, place, a_ref, b_ref, w_ref, m_ref, *outs):
    width = m_ref.shape[2]
    for (turn, first), out in zip(parts, outs, strict=True):
        chip = lax.rem(place[0] + turn, NY)
        column = pl.multiple_of((2 * chip + place[1]) * width, width)
        here = slice(first, first + rows)
        total = jnp.dot(
            a_ref[here], w_ref[:, pl.ds(column, width)], preferred_element_type=jnp.float32
        )
        total += jnp.dot(b_ref[here], m_ref[chip], preferred_element_type=jnp.float32)
        out[...] = total.astype(jnp.bfloat16)


def project(place, mine, mate, w_out, w_mate, parts, rows):
    depth, width = w_mate.shape[1:]
    vmem = pl.BlockSpec(memory_space=pltpu.VMEM)
    return pl.pallas_call(
        functools.partial(project_kernel, parts, rows),
        out_shape=[jax.ShapeDtypeStruct((rows, width), jnp.bfloat16)] * len(parts),
        in_specs=[pl.BlockSpec(memory_space=pltpu.SMEM)] + [vmem] * 4,
        out_specs=[vmem] * len(parts),
        compiler_params=pltpu.CompilerParams(vmem_limit_bytes=10 * MIB),
        cost_estimate=pl.CostEstimate(
            flops=4 * rows * len(parts) * depth * width,
            bytes_accessed=4 * MIB,
            transcendentals=0,
        ),
    )(place, mine, mate, w_out, w_mate)


def final_kernel(suffix, chunks, order, *refs):
    o_ref = refs[-1]
    at = 0
    for lo, terms in chunks:
        own, *halves = refs[at : at + terms]
        at += terms
        half = halves[0].shape[0]
        for n in range(own.shape[0] // suffix):
            row = n * suffix
            first, second = halves[:2] if row < half else halves[2:]
            here = slice(row % half, row % half + suffix)
            total = own[row : row + suffix].astype(jnp.float32) + first[here] + second[here]
            o_ref[order[lo + n]] = total.astype(jnp.bfloat16)


def again_kernel(suffix, chunks, order, *refs):
    refs[-1][...] = refs[-2][...]
    final_kernel(suffix, chunks, order, *refs[:-2], refs[-1])


def added(*terms):
    return sum(t.astype(jnp.float32) for t in terms).astype(jnp.bfloat16)


EARLY = [
    dz * NX + dx
    for dz, dx in [(0, 0), (1, 0), (7, 0), (0, 1), (0, 3), (2, 0), (6, 0), (0, 2), (3, 0), (5, 0)]
    + [(4, 0)]
    + [(dz, dx) for dz in (1, 7, 2, 6) for dx in (1, 3, 2)]
]
PLACES = EARLY + [code for code in range(NX * NZ) if code not in EARLY]


class Projection:
    def __init__(self, place, w_out, w_mate, mine, mate):
        self.part = functools.partial(project, place, mine, mate, w_out, w_mate)
        self.rows = mine.shape[0]

    def first(self):
        half = self.rows // 2
        top2, low2 = self.part([(2, 0), (2, half)], half)
        top2, low2 = send_y(top2, 1), send_y(low2, -1)
        low1, top3, own_top1, own_low3 = self.part(
            [(1, half), (3, 0), (1, 0), (3, half)], half
        )
        self.low1, self.top3 = send_y(low1, 1), send_y(top3, -1)
        return added(own_top1, top2), added(own_low3, low2)

    def second(self, top1, low3):
        top1, low3 = send_y(top1, 1), send_y(low3, -1)
        (own,) = self.part([(0, 0)], self.rows)
        return own, top1, self.top3, self.low1, low3


def shards(queries, prefix_kv, suffix_kv, candidate_prefix, w_out):
    count, suffix, width = queries.shape
    length = prefix_kv.shape[2]
    out_width = w_out.shape[1] // (2 * NY)
    chunk = count // 2
    me = lax.axis_index("cache")
    t = lax.axis_index("tensor")
    place = jnp.stack([t // 2, t % 2]).astype(jnp.int32)

    ids = candidate_prefix[:, 0]
    codes = ((ids % NZ - me % NZ) % NZ) * NX + (ids // NZ - me // NZ) % NX
    arrival = sum(
        jnp.where(codes == code, at, 0) for at, code in enumerate(PLACES)
    )
    number = jnp.arange(count, dtype=jnp.int32)
    key = arrival.astype(jnp.int32) * count + number
    rank = jnp.sum((key[None, :] < key[:, None]).astype(jnp.int32), axis=1)
    order = jnp.sum(jnp.where(rank[:, None] == number[None, :], number[:, None], 0), axis=0)
    early = jnp.sum((arrival < len(EARLY)).astype(jnp.int32)).reshape(1)

    vmem = pl.BlockSpec(memory_space=pltpu.VMEM)
    smem = pl.BlockSpec(memory_space=pltpu.SMEM)
    out_shape = jax.ShapeDtypeStruct((count, suffix, out_width), jnp.bfloat16)
    limit = pltpu.CompilerParams(vmem_limit_bytes=10 * MIB)

    gather = Gather(prefix_kv.reshape(2, length, HD))
    w_mate = swap_core(pick_columns(place, w_out, out_width))

    sources = gather.early()
    (mine,) = attend(
        order, codes, early, queries, suffix_kv, sources, 0, chunk, length, False
    )
    gather.late()
    mine = mine.reshape(chunk * suffix, width)
    mate = swap_core(mine)
    mate, sources = gather.last(mate)
    one = Projection(place, w_out, w_mate, mine, mate)
    top1, low3 = one.first()

    top1, low3, queries = together(top1, low3, queries)
    mine, again = attend(
        order, codes, early, queries, suffix_kv, sources, chunk, chunk, length, True
    )
    mine = mine.reshape(chunk * suffix, width)
    mate = swap_core(mine)
    own, top1, top3, low1, low3 = one.second(top1, low3)
    mate, top1, top3, low1, low3 = together(mate, top1, top3, low1, low3)
    terms = [own, top1, top3, low1, low3]
    two = Projection(place, w_out, w_mate, mine, mate)
    terms += two.second(*two.first())
    out = pl.pallas_call(
        functools.partial(final_kernel, suffix, [(0, 5), (chunk, 5)]),
        out_shape=out_shape,
        in_specs=[smem] + [vmem] * 10,
        out_specs=vmem,
        compiler_params=limit,
    )(order, *terms)

    def redo(state):
        step, out = state
        mine = again.reshape(chunk * suffix, width)
        extra = Projection(place, w_out, w_mate, mine, swap_core(mine))
        terms = extra.second(*extra.first())
        out = pl.pallas_call(
            functools.partial(again_kernel, suffix, [(0, 5)]),
            out_shape=out_shape,
            in_specs=[smem] + [vmem] * 6,
            out_specs=vmem,
            compiler_params=limit,
        )(order, *terms, out)
        return step + 1, out

    wrong = (early[0] < chunk).astype(jnp.int32)
    return lax.while_loop(lambda state: state[0] < wrong, redo, (jnp.int32(0), out))[1]


def solution(mesh):
    in_specs = (
        P("cache", None, "tensor"),
        P(None, "cache", None, "tensor"),
        P(None, "cache", None, "tensor"),
        P("cache", None),
        P("tensor", None),
    )
    out_specs = P("cache", None, "tensor")
    return jax.shard_map(shards, mesh=mesh, in_specs=in_specs, out_specs=out_specs, check_vma=False)
```

```python
import functools
import math

import jax
import jax.numpy as jnp
from jax import lax
from jax.experimental import pallas as pl
from jax.experimental.pallas import tpu as pltpu
from jax.sharding import PartitionSpec as P

H = 64
KVH = 8
HD = 128
GROUP = H // KVH
NX = 4
NZ = 8
NY = 4
LOG2E = 1.4426950408889634
MIB = 1024 * 1024


def send_cache(value, step_x, step_z):
    pairs = [
        (x * NZ + z, ((x + step_x) % NX) * NZ + (z + step_z) % NZ)
        for x in range(NX)
        for z in range(NZ)
    ]
    return lax.ppermute(value, "cache", pairs)


def send_y(value, step):
    pairs = [(2 * y + c, 2 * ((y + step) % NY) + c) for y in range(NY) for c in range(2)]
    return lax.ppermute(value, "tensor", pairs)


def swap_core(value):
    return lax.ppermute(value, "tensor", [(t, t ^ 1) for t in range(2 * NY)])


def together(*values):
    return lax.optimization_barrier(values)


class Gather:
    def __init__(self, block):
        self.block = block
        self.half = block.shape[1] // 2
        self.sources = {}

    def part(self, array, at, kv, dz, dx, first=0):
        code = (dz % NZ) * NX + dx % NX
        self.sources.setdefault(code, []).append((array, at, kv, first))

    def whole(self, array, dz, dx):
        for kv in range(2):
            self.part(array, kv, kv, dz, dx)

    def early(self):
        block = self.block
        z1a, z1b = send_cache(block, 0, -1), send_cache(block, 0, 1)
        x1a, x1b = send_cache(block, -1, 0), send_cache(block, 1, 0)
        self.begun = z1a, z1b, x1a, x1b
        z2a, z2b = send_cache(z1a, 0, -1), send_cache(z1b, 0, 1)
        key_x2, value_x2 = send_cache(x1a[0:1], -1, 0), send_cache(x1b[1:2], 1, 0)
        values = jnp.concatenate([x1a[1:2], x1b[1:2], value_x2], axis=0)
        near = jnp.concatenate([z1a[0:1], z1b[0:1], z2a[0:1], z2b[0:1]], axis=0)
        near_a, near_b = send_cache(near, -1, 0), send_cache(near, 1, 0)
        z3a, z3b = send_cache(z2a, 0, -1), send_cache(z2b, 0, 1)
        v1a, v1b = send_cache(values, 0, -1), send_cache(values, 0, 1)
        v1a, v1b, near_a, near_b, z3a, z3b = together(v1a, v1b, near_a, near_b, z3a, z3b)
        key_z4, value_z4 = send_cache(z3a[0:1], 0, -1), send_cache(z3b[1:2], 0, 1)
        near_c, near_d = send_cache(near_a[:2], -1, 0), send_cache(near_b[2:], 1, 0)
        v2a, v2b = send_cache(v1a, 0, -1), send_cache(v1b, 0, 1)
        v2a, v2b, near_c, near_d, key_z4, value_z4 = together(
            v2a, v2b, near_c, near_d, key_z4, value_z4
        )
        self.whole(block, 0, 0)
        for step, ahead, behind in ((1, z1a, z1b), (2, z2a, z2b), (3, z3a, z3b)):
            self.whole(ahead, step, 0)
            self.whole(behind, -step, 0)
        self.part(key_z4, 0, 0, 4, 0)
        self.part(value_z4, 0, 1, 4, 0)
        self.whole(x1a, 0, 1)
        self.whole(x1b, 0, -1)
        self.part(key_x2, 0, 0, 0, 2)
        self.part(value_x2, 0, 1, 0, 2)
        for at, dx in enumerate((1, -1, 2)):
            for step, ahead, behind in ((1, v1a, v1b), (2, v2a, v2b)):
                self.part(ahead, at, 1, step, dx)
                self.part(behind, at, 1, -step, dx)
        for at, dz in enumerate((1, -1, 2, -2)):
            self.part(near_a, at, 0, dz, 1)
            self.part(near_b, at, 0, dz, -1)
            self.part(near_c if at < 2 else near_d, at % 2, 0, dz, 2)
        self.distant = [z3a[0:1], z3b[0:1], key_z4]
        self.values = v2a, v2b
        return {code: list(parts) for code, parts in self.sources.items()}

    def late(self):
        v2a, v2b = self.values
        distant = jnp.concatenate(self.distant, axis=0)
        v3a, v3b = send_cache(v2a, 0, -1), send_cache(v2b, 0, 1)
        far_a, far_b = send_cache(distant, -1, 0), send_cache(distant, 1, 0)
        self.hop = v3a, v3b, far_a, far_b

    def last(self, token):
        token, v3a, v3b, far_a, far_b = together(token, *self.hop)
        self.values = self.distant = None
        half = self.half
        v4a, v4b = send_cache(v3a[:, :half], 0, -1), send_cache(v3b[:, half:], 0, 1)
        far_c, far_d = send_cache(far_a[:, :half], -1, 0), send_cache(far_b[:, half:], 1, 0)
        for at, dx in enumerate((1, -1, 2)):
            self.part(v3a, at, 1, 3, dx)
            self.part(v3b, at, 1, -3, dx)
            self.part(v4a, at, 1, 4, dx, 0)
            self.part(v4b, at, 1, 4, dx, half)
        for at, dz in enumerate((3, -3, 4)):
            self.part(far_a, at, 0, dz, 1)
            self.part(far_b, at, 0, dz, -1)
            self.part(far_c, at, 0, dz, 2, 0)
            self.part(far_d, at, 0, dz, 2, half)
        return token, self.sources


LAST = (((1,), (1,)), ((), ()))
INNER = (((1,), (0,)), ((), ()))


def beside_ones(values):
    return jnp.concatenate([values, jnp.ones_like(values)], axis=1)


def plan_kernel(ids, order, codes, info):
    me = lax.axis_index("cache")
    t = lax.axis_index("tensor")
    count = ids.shape[0]
    info[0] = t // 2
    info[1] = t % 2

    def is_early(code):
        dz = code // NX
        return (code % NX == 0) | (dz <= 2) | (dz >= NZ - 2)

    def first(n, at):
        passage = ids[n, 0]
        dz = (passage % NZ - me % NZ + NZ) % NZ
        dx = (passage // NZ - me // NZ + NX) % NX
        code = dz * NX + dx
        codes[n] = code
        order[at] = n
        return at + is_early(code).astype(jnp.int32)

    early = lax.fori_loop(0, count, first, jnp.int32(0))
    info[2] = early

    def second(n, at):
        late = jnp.logical_not(is_early(codes[n]))

        @pl.when(late)
        def _():
            order[at] = n

        return at + late.astype(jnp.int32)

    lax.fori_loop(0, count, second, early)


def plan(candidate_prefix):
    count = candidate_prefix.shape[0]
    smem = pl.BlockSpec(memory_space=pltpu.SMEM)
    return pl.pallas_call(
        plan_kernel,
        out_shape=[jax.ShapeDtypeStruct((n,), jnp.int32) for n in (count, count, 3)],
        in_specs=[smem],
        out_specs=[smem] * 3,
        compiler_params=pltpu.CompilerParams(vmem_limit_bytes=MIB),
        cost_estimate=pl.CostEstimate(flops=1000, bytes_accessed=1000, transcendentals=0),
    )(candidate_prefix)


def attention_kernel(sources, n_arrays, lo, count, batch, order, codes, info, q_ref, s_ref, *rest):
    arrays = rest[:n_arrays]
    *outs, cache = rest[n_arrays:]
    suffix = q_ref.shape[1]
    rows = GROUP * suffix
    factor = LOG2E / math.sqrt(HD)
    token = lax.broadcasted_iota(jnp.int32, (rows, HD), 0) % suffix
    causal = lax.broadcasted_iota(jnp.int32, (rows, HD), 1) <= token
    blank = jnp.zeros((HD - suffix, HD), jnp.bfloat16)

    def fetch(first):
        @pl.loop(0, batch)
        def _(i):
            code = codes[order[first + i]]
            for dx in range(NX):

                @pl.when(code % NX == dx)
                def _(dx=dx):
                    for dz in range(NZ):
                        parts = sources.get(dz * NX + dx)
                        if parts is None:
                            continue

                        @pl.when(code // NX == dz)
                        def _(parts=parts):
                            for which, at, kv, row in parts:
                                block = arrays[which][at]
                                cache[i, kv, row : row + block.shape[0]] = block

    def attend_batch(first, at, out):
        fetch(first)
        scores = []
        for i in range(batch):
            n = order[first + i]
            q = jnp.concatenate([q_ref[n, :, g * HD : (g + 1) * HD] for g in range(GROUP)], axis=0)
            far = lax.dot_general(q, cache[i, 0], LAST, preferred_element_type=jnp.float32)
            keys = jnp.concatenate([s_ref[0, n], blank], axis=0)
            near = lax.dot_general(q, keys, LAST, preferred_element_type=jnp.float32)
            near = jnp.where(causal, near, -jnp.inf)
            scores.append([far[:, j : j + HD] for j in range(0, far.shape[1], HD)] + [near])
        weights = []
        for tiles in scores:
            top = jnp.max(functools.reduce(jnp.maximum, tiles), axis=1, keepdims=True)
            weights.append([jnp.exp2((s - top) * factor).astype(jnp.bfloat16) for s in tiles])
        for i in range(batch):
            n = order[first + i]
            far = jnp.concatenate(weights[i][:-1], axis=1)
            near = weights[i][-1][:, :suffix]
            summed = lax.dot_general(
                far, beside_ones(cache[i, 1]), INNER, preferred_element_type=jnp.float32
            ) + lax.dot_general(
                near, beside_ones(s_ref[1, n]), INNER, preferred_element_type=jnp.float32
            )
            result = (summed[:, :HD] / summed[:, HD:]).astype(jnp.bfloat16)
            for g in range(GROUP):
                out[at + i, :, g * HD : (g + 1) * HD] = result[g * suffix : (g + 1) * suffix]

    @pl.loop(0, count // batch)
    def _(step):
        attend_batch(lo + step * batch, step * batch, outs[0])

    if len(outs) > 1:
        @pl.loop(0, jnp.where(info[2] < lo, count // batch, 0))
        def _(step):
            attend_batch(step * batch, step * batch, outs[1])


def attend(order, codes, info, queries, suffix_kv, sources, lo, count, length, again):
    arrays = []
    places = {}
    for code, parts in sources.items():
        for array, at, kv, first in parts:
            which = next((n for n, a in enumerate(arrays) if a is array), len(arrays))
            if which == len(arrays):
                arrays.append(array)
            places.setdefault(code, []).append((which, at, kv, first))
    _, suffix, width = queries.shape
    batch = 4
    vmem = pl.BlockSpec(memory_space=pltpu.VMEM)
    smem = pl.BlockSpec(memory_space=pltpu.SMEM)
    shape = jax.ShapeDtypeStruct((count, suffix, width), jnp.bfloat16)
    outs = 2 if again else 1
    return pl.pallas_call(
        functools.partial(attention_kernel, places, len(arrays), lo, count, batch),
        out_shape=[shape] * outs,
        in_specs=[smem] * 3 + [vmem] * (2 + len(arrays)),
        out_specs=[vmem] * outs,
        scratch_shapes=[pltpu.VMEM((batch, 2, length, HD), jnp.bfloat16)],
        compiler_params=pltpu.CompilerParams(vmem_limit_bytes=24 * MIB),
        cost_estimate=pl.CostEstimate(
            flops=4 * count * suffix * width * length,
            bytes_accessed=8 * MIB,
            transcendentals=count * suffix * GROUP * length,
        ),
    )(order, codes, info, queries, suffix_kv, *arrays)


def pick_kernel(place, w_ref, o_ref):
    o_ref[0] = w_ref[...]


def pick_columns(place, w_out, width):
    depth = w_out.shape[0]
    return pl.pallas_call(
        pick_kernel,
        out_shape=jax.ShapeDtypeStruct((NY, depth, width), w_out.dtype),
        grid_spec=pltpu.PrefetchScalarGridSpec(
            num_scalar_prefetch=1,
            grid=(NY,),
            in_specs=[pl.BlockSpec((depth, width), lambda n, p: (0, 2 * n + 1 - p[1]))],
            out_specs=pl.BlockSpec((1, depth, width), lambda n, p: (n, 0, 0)),
        ),
        compiler_params=pltpu.CompilerParams(vmem_limit_bytes=8 * MIB),
        cost_estimate=pl.CostEstimate(flops=0, bytes_accessed=8 * MIB, transcendentals=0),
    )(place, w_out)


def project_kernel(turns, place, a_ref, b_ref, w_ref, m_ref, *outs):
    width = m_ref.shape[2]
    half = a_ref.shape[0] // 2
    for at, turn in enumerate(turns):
        chip = lax.rem(place[0] + turn, NY)
        column = pl.multiple_of((2 * chip + place[1]) * width, width)
        total = jnp.dot(
            a_ref[...], w_ref[:, pl.ds(column, width)], preferred_element_type=jnp.float32
        )
        total += jnp.dot(b_ref[...], m_ref[chip], preferred_element_type=jnp.float32)
        total = total.astype(jnp.bfloat16)
        outs[2 * at][...] = total[:half]
        outs[2 * at + 1][...] = total[half:]


def project(place, mine, mate, w_out, w_mate, turns):
    depth, width = w_mate.shape[1:]
    rows = mine.shape[0]
    vmem = pl.BlockSpec(memory_space=pltpu.VMEM)
    count = 2 * len(turns)
    return pl.pallas_call(
        functools.partial(project_kernel, turns),
        out_shape=[jax.ShapeDtypeStruct((rows // 2, width), jnp.bfloat16)] * count,
        in_specs=[pl.BlockSpec(memory_space=pltpu.SMEM)] + [vmem] * 4,
        out_specs=[vmem] * count,
        compiler_params=pltpu.CompilerParams(vmem_limit_bytes=26 * MIB),
        cost_estimate=pl.CostEstimate(
            flops=4 * rows * len(turns) * depth * width,
            bytes_accessed=4 * MIB,
            transcendentals=0,
        ),
    )(place, mine, mate, w_out, w_mate)


def final_kernel(suffix, chunks, order, *refs):
    o_ref = refs[-1]
    for lo, at in chunks:
        for side, terms in enumerate((refs[at : at + 3], refs[at + 3 : at + 6])):
            each = terms[0].shape[0] // suffix
            for n in range(each):
                here = slice(n * suffix, (n + 1) * suffix)
                total = sum(term[here].astype(jnp.float32) for term in terms)
                o_ref[order[lo + side * each + n]] = total.astype(jnp.bfloat16)


def again_kernel(suffix, chunks, order, *refs):
    refs[-1][...] = refs[-2][...]
    final_kernel(suffix, chunks, order, *refs[:-2], refs[-1])


def added(*terms):
    return sum(t.astype(jnp.float32) for t in terms).astype(jnp.bfloat16)


class Projection:
    def __init__(self, place, w_out, w_mate, mine, mate):
        self.part = functools.partial(project, place, mine, mate, w_out, w_mate)

    def first(self):
        top2, low2 = self.part((2,))
        top2, low2 = send_y(top2, 1), send_y(low2, -1)
        top1, low1, top3, low3 = self.part((1, 3))
        self.low1, self.top3 = send_y(low1, 1), send_y(top3, -1)
        return added(top1, top2), added(low3, low2)

    def second(self, top1, low3):
        self.top1, self.low3 = send_y(top1, 1), send_y(low3, -1)

    def terms(self):
        own_top, own_low = self.part((0,))
        return [own_top, self.top1, self.top3, own_low, self.low1, self.low3]


def shards(queries, prefix_kv, suffix_kv, candidate_prefix, w_out):
    count, suffix, width = queries.shape
    length = prefix_kv.shape[2]
    out_width = w_out.shape[1] // (2 * NY)
    chunk = count // 2
    order, codes, info = plan(candidate_prefix)

    vmem = pl.BlockSpec(memory_space=pltpu.VMEM)
    smem = pl.BlockSpec(memory_space=pltpu.SMEM)
    out_shape = jax.ShapeDtypeStruct((count, suffix, out_width), jnp.bfloat16)
    limit = pltpu.CompilerParams(vmem_limit_bytes=12 * MIB)

    gather = Gather(prefix_kv.reshape(2, length, HD))
    sources = gather.early()
    later, *_ = together(info, *gather.begun)
    w_mate = swap_core(pick_columns(later, w_out, out_width))

    (mine,) = attend(order, codes, info, queries, suffix_kv, sources, 0, chunk, length, False)
    gather.late()
    mine, sources = gather.last(mine.reshape(chunk * suffix, width))
    one = Projection(info, w_out, w_mate, mine, swap_core(mine))
    top1, low3 = one.first()

    top1, low3, order2 = together(top1, low3, order)
    mine, again = attend(
        order2, codes, info, queries, suffix_kv, sources, chunk, chunk, length, True
    )
    mine = mine.reshape(chunk * suffix, width)
    mate = swap_core(mine)
    one.second(top1, low3)
    mate, one.top1, one.top3, one.low1, one.low3 = together(
        mate, one.top1, one.top3, one.low1, one.low3
    )
    two = Projection(info, w_out, w_mate, mine, mate)
    two.second(*two.first())
    out = pl.pallas_call(
        functools.partial(final_kernel, suffix, [(0, 0), (chunk, 6)]),
        out_shape=out_shape,
        in_specs=[smem] + [vmem] * 12,
        out_specs=vmem,
        compiler_params=limit,
    )(order, *one.terms(), *two.terms())

    def redo(state):
        left, out, again = state
        mine = again.reshape(chunk * suffix, width)
        extra = Projection(info, w_out, w_mate, mine, swap_core(mine))
        extra.second(*extra.first())
        out = pl.pallas_call(
            functools.partial(again_kernel, suffix, [(0, 0)]),
            out_shape=out_shape,
            in_specs=[smem] + [vmem] * 7,
            out_specs=vmem,
            compiler_params=limit,
        )(order, *extra.terms(), out)
        again, out = together(again, out)
        return left - 1, out, again

    left = (info[2] < chunk).astype(jnp.int32)
    return lax.while_loop(lambda state: state[0] > 0, redo, (left, out, again))[1]


def solution(mesh):
    in_specs = (
        P("cache", None, "tensor"),
        P(None, "cache", None, "tensor"),
        P(None, "cache", None, "tensor"),
        P("cache", None),
        P("tensor", None),
    )
    out_specs = P("cache", None, "tensor")
    return jax.shard_map(shards, mesh=mesh, in_specs=in_specs, out_specs=out_specs, check_vma=False)
```

```python
import functools
import math

import jax
import jax.numpy as jnp
from jax import lax
from jax.experimental import pallas as pl
from jax.experimental.pallas import tpu as pltpu
from jax.sharding import PartitionSpec as P

H = 64
KVH = 8
HD = 128
GROUP = H // KVH
NX = 4
NZ = 8
NY = 4
LOG2E = 1.4426950408889634
MIB = 1024 * 1024


def send_cache(value, along_z):
    pairs = []
    for x in range(NX):
        for z in range(NZ):
            for t in range(2 * NY):
                step = -1 if t % 2 else 1
                to_x, to_z = (x, (z + step) % NZ) if along_z else ((x + step) % NX, z)
                pairs.append(((x * NZ + z) * 2 * NY + t, (to_x * NZ + to_z) * 2 * NY + t))
    return lax.ppermute(value, ("cache", "tensor"), pairs)


def send_y(value, step):
    pairs = [(2 * y + c, 2 * ((y + step) % NY) + c) for y in range(NY) for c in range(2)]
    return lax.ppermute(value, "tensor", pairs)


def swap_core(value):
    return lax.ppermute(value, "tensor", [(t, t ^ 1) for t in range(2 * NY)])


def together(*values):
    return lax.optimization_barrier(values)


def pack_kernel(places, n_arrays, *refs):
    o_ref = refs[n_arrays]
    for index, (which, at) in places:
        o_ref[index] = refs[which][at]


def pack(parts):
    arrays = []
    places = []
    for i, row in enumerate(parts):
        for j, (array, at) in enumerate(row):
            which = next((n for n, a in enumerate(arrays) if a is array), len(arrays))
            if which == len(arrays):
                arrays.append(array)
            places.append(((i, j), (which, at)))
    block = arrays[0].shape[-2:]
    vmem = pl.BlockSpec(memory_space=pltpu.VMEM)
    return pl.pallas_call(
        functools.partial(pack_kernel, places, len(arrays)),
        out_shape=jax.ShapeDtypeStruct((len(parts), len(parts[0])) + block, jnp.bfloat16),
        in_specs=[vmem] * len(arrays),
        out_specs=vmem,
        compiler_params=pltpu.CompilerParams(vmem_limit_bytes=6 * MIB),
        cost_estimate=pl.CostEstimate(flops=0, bytes_accessed=MIB, transcendentals=0),
    )(*arrays)


class Gather:
    def __init__(self, block):
        self.block = block
        self.sources = {}

    def part(self, array, at, kv, dz, dx):
        code = (dz % NZ) * NX + dx % NX
        self.sources.setdefault(code, []).append((array, at, kv))

    def whole(self, array, at, dz, dx):
        for kv in range(2):
            self.part(array, at + (kv,), kv, dz, dx)

    def early(self, *tokens):
        block = self.block
        other = swap_core(block)
        both = pack([[(block, 0), (block, 1)], [(other, 0), (other, 1)]])
        x1, z1 = send_cache(both, False), send_cache(both, True)
        x1, z1, *tokens = together(x1, z1, *tokens)
        x1m, z1m = swap_core(x1), swap_core(z1)
        x2, z2 = send_cache(x1, False), send_cache(z1, True)
        x2, z2, x1m, z1m = together(x2, z2, x1m, z1m)
        values = pack(
            [
                [(x1, (0, 1)), (x1m, (1, 1)), (x2, (0, 1))],
                [(x1, (1, 1)), (x1m, (0, 1)), (x2, (1, 1))],
            ]
        )
        z2m = swap_core(z2)
        near = pack(
            [
                [(z1, (0, 0)), (z1m, (1, 0)), (z2, (0, 0)), (z2m, (1, 0))],
                [(z1, (1, 0)), (z1m, (0, 0)), (z2, (1, 0)), (z2m, (0, 0))],
            ]
        )
        v1, n1 = send_cache(values, True), send_cache(near, False)
        z3 = send_cache(z2, True)
        v1, n1, z3 = together(v1, n1, z3)
        z3m, n1m, v1m = swap_core(z3), swap_core(n1[1]), swap_core(v1[1])
        z4, n2, v2 = send_cache(z3[0], True), send_cache(n1[0], False), send_cache(v1, True)
        z4, n2, v2, z3m, n1m, v1m = together(z4, n2, v2, z3m, n1m, v1m)
        v2m = swap_core(v2[1])

        self.whole(block, (), 0, 0)
        self.whole(x1, (0,), 0, 1)
        self.whole(x1m, (1,), 0, -1)
        self.whole(x2, (0,), 0, 2)
        for step, mine, mate in ((1, z1, z1m), (2, z2, z2m), (3, z3, z3m)):
            self.whole(mine, (0,), step, 0)
            self.whole(mate, (1,), -step, 0)
        self.whole(z4, (), 4, 0)
        for step, mine, mate in ((1, v1, v1m), (2, v2, v2m)):
            self.values(mine, mate, step)
        for at, dz in enumerate((1, -1, 2, -2)):
            self.part(n1, (0, at), 0, dz, 1)
            self.part(n1m, (at,), 0, -dz, -1)
            self.part(n2, (at,), 0, dz, 2)
        self.left = v2, z3, z3m, z4
        return tokens, {code: list(parts) for code, parts in self.sources.items()}

    def values(self, mine, mate, step):
        for at, dx in enumerate((1, -1, 2)):
            self.part(mine, (0, at), 1, step, dx)
            self.part(mate, (at,), 1, -step, -dx)

    def late(self):
        v2, z3, z3m, z4 = self.left
        key_z4m = swap_core(z4[0:1])
        distant = pack(
            [
                [(z3, (0, 0)), (z3m, (1, 0)), (z4, 0)],
                [(z3, (1, 0)), (z3m, (0, 0)), (key_z4m, 0)],
            ]
        )
        self.hop = send_cache(v2, True), send_cache(distant, False)

    def last(self, token):
        token, v3, f1 = together(token, *self.hop)
        v4, f2 = send_cache(v3[0], True), send_cache(f1[0], False)
        self.final = v3, f1, v4, f2
        return token

    def finish(self, *tokens):
        count = len(tokens)
        done = together(*tokens, *self.final)
        v3, f1, v4, f2 = done[count:]
        third = range(3)
        rest = swap_core(pack([[(v3, (1, at)) for at in third], [(f1, (1, at)) for at in third]]))
        for at, dx in enumerate((1, -1, 2)):
            self.part(v3, (0, at), 1, 3, dx)
            self.part(rest, (0, at), 1, -3, -dx)
            self.part(v4, (at,), 1, 4, dx)
        for at, dz in enumerate((3, -3, 4)):
            self.part(f1, (0, at), 0, dz, 1)
            self.part(rest, (1, at), 0, -dz, -1)
            self.part(f2, (at,), 0, dz, 2)
        return done[:count], self.sources


LAST = (((1,), (1,)), ((), ()))
INNER = (((1,), (0,)), ((), ()))


def beside_ones(values):
    return jnp.concatenate([values, jnp.ones_like(values)], axis=1)


def plan_kernel(ids, order, codes, info):
    me = lax.axis_index("cache")
    t = lax.axis_index("tensor")
    count = ids.shape[0]
    info[0] = t // 2
    info[1] = t % 2

    def is_early(code):
        dz = code // NX
        return (code % NX == 0) | (dz <= 2) | (dz >= NZ - 2)

    def first(n, at):
        passage = ids[n]
        dz = (passage % NZ - me % NZ + NZ) % NZ
        dx = (passage // NZ - me // NZ + NX) % NX
        dz = jnp.where(t % 2 == 0, (NZ - dz) % NZ, dz)
        dx = jnp.where(t % 2 == 0, (NX - dx) % NX, dx)
        code = dz * NX + dx
        codes[n] = code
        order[at] = n
        return at + is_early(code).astype(jnp.int32)

    early = lax.fori_loop(0, count, first, jnp.int32(0))
    info[2] = early

    def second(n, at):
        late = jnp.logical_not(is_early(codes[n]))

        @pl.when(late)
        def _():
            order[at] = n

        return at + late.astype(jnp.int32)

    lax.fori_loop(0, count, second, early)


def plan(candidate_prefix):
    count = candidate_prefix.shape[0]
    smem = pl.BlockSpec(memory_space=pltpu.SMEM)
    return pl.pallas_call(
        plan_kernel,
        out_shape=[jax.ShapeDtypeStruct((n,), jnp.int32) for n in (count, count, 3)],
        in_specs=[smem],
        out_specs=[smem] * 3,
        compiler_params=pltpu.CompilerParams(vmem_limit_bytes=MIB),
        cost_estimate=pl.CostEstimate(flops=1000, bytes_accessed=1000, transcendentals=0),
    )(candidate_prefix.reshape(count))


def attention_kernel(sources, n_arrays, lo, count, batch, order, codes, info, q_ref, s_ref, *rest):
    arrays = rest[:n_arrays]
    *outs, cache = rest[n_arrays:]
    suffix = q_ref.shape[1]
    rows = GROUP * suffix
    factor = LOG2E / math.sqrt(HD)
    token = lax.broadcasted_iota(jnp.int32, (rows, HD), 0) % suffix
    causal = lax.broadcasted_iota(jnp.int32, (rows, HD), 1) <= token
    blank = jnp.zeros((HD - suffix, HD), jnp.bfloat16)

    def fetch(first):
        @pl.loop(0, batch)
        def _(i):
            code = codes[order[first + i]]
            for dx in range(NX):

                @pl.when(code % NX == dx)
                def _(dx=dx):
                    for dz in range(NZ):
                        parts = sources.get(dz * NX + dx)
                        if parts is None:
                            continue

                        @pl.when(code // NX == dz)
                        def _(parts=parts):
                            for which, at, kv in parts:
                                cache[i, kv] = arrays[which][at]

    def attend_batch(first, at, out):
        fetch(first)
        scores = []
        for i in range(batch):
            n = order[first + i]
            q = jnp.concatenate([q_ref[n, :, g * HD : (g + 1) * HD] for g in range(GROUP)], axis=0)
            far = lax.dot_general(q, cache[i, 0], LAST, preferred_element_type=jnp.float32)
            keys = jnp.concatenate([s_ref[0, n], blank], axis=0)
            near = lax.dot_general(q, keys, LAST, preferred_element_type=jnp.float32)
            near = jnp.where(causal, near, -jnp.inf)
            scores.append([far[:, j : j + HD] for j in range(0, far.shape[1], HD)] + [near])
        weights = []
        for tiles in scores:
            top = jnp.max(functools.reduce(jnp.maximum, tiles), axis=1, keepdims=True)
            weights.append([jnp.exp2((s - top) * factor).astype(jnp.bfloat16) for s in tiles])
        for i in range(batch):
            n = order[first + i]
            far = jnp.concatenate(weights[i][:-1], axis=1)
            near = weights[i][-1][:, :suffix]
            summed = lax.dot_general(
                far, beside_ones(cache[i, 1]), INNER, preferred_element_type=jnp.float32
            ) + lax.dot_general(
                near, beside_ones(s_ref[1, n]), INNER, preferred_element_type=jnp.float32
            )
            result = (summed[:, :HD] / summed[:, HD:]).astype(jnp.bfloat16)
            for g in range(GROUP):
                out[at + i, :, g * HD : (g + 1) * HD] = result[g * suffix : (g + 1) * suffix]

    @pl.loop(0, count // batch)
    def _(step):
        attend_batch(lo + step * batch, step * batch, outs[0])

    if len(outs) > 1:
        @pl.loop(0, jnp.where(info[2] < lo, count // batch, 0))
        def _(step):
            attend_batch(step * batch, step * batch, outs[1])


def attend(order, codes, info, queries, suffix_kv, sources, lo, count, length, again):
    arrays = []
    places = {}
    for code, parts in sources.items():
        for array, at, kv in parts:
            which = next((n for n, a in enumerate(arrays) if a is array), len(arrays))
            if which == len(arrays):
                arrays.append(array)
            places.setdefault(code, []).append((which, at, kv))
    _, suffix, width = queries.shape
    batch = 4
    vmem = pl.BlockSpec(memory_space=pltpu.VMEM)
    smem = pl.BlockSpec(memory_space=pltpu.SMEM)
    shape = jax.ShapeDtypeStruct((count, suffix, width), jnp.bfloat16)
    outs = 2 if again else 1
    return pl.pallas_call(
        functools.partial(attention_kernel, places, len(arrays), lo, count, batch),
        out_shape=[shape] * outs,
        in_specs=[smem] * 3 + [vmem] * (2 + len(arrays)),
        out_specs=[vmem] * outs,
        scratch_shapes=[pltpu.VMEM((batch, 2, length, HD), jnp.bfloat16)],
        compiler_params=pltpu.CompilerParams(vmem_limit_bytes=28 * MIB),
        cost_estimate=pl.CostEstimate(
            flops=4 * count * suffix * width * length,
            bytes_accessed=8 * MIB,
            transcendentals=count * suffix * GROUP * length,
        ),
    )(order, codes, info, queries, suffix_kv, *arrays)


def columns_of(place, turn, other, width):
    core = 1 - place[1] if other else place[1]
    return pl.multiple_of((2 * lax.rem(place[0] + turn, NY) + core) * width, width)


def project_other_kernel(turns, place, a_ref, w_ref, o_ref):
    width = o_ref.shape[2]
    for at, turn in enumerate(turns):
        column = columns_of(place, turn, True, width)
        total = jnp.dot(
            a_ref[...], w_ref[:, pl.ds(column, width)], preferred_element_type=jnp.float32
        )
        o_ref[at] = total.astype(jnp.bfloat16)


def project_own_kernel(turns, first, split, place, a_ref, w_ref, came_ref, *outs):
    width = came_ref.shape[2]
    half = a_ref.shape[0] // 2
    for at, turn in enumerate(turns):
        column = columns_of(place, turn, False, width)
        total = jnp.dot(
            a_ref[...], w_ref[:, pl.ds(column, width)], preferred_element_type=jnp.float32
        )
        total = (total + came_ref[first + at].astype(jnp.float32)).astype(jnp.bfloat16)
        if split:
            outs[2 * at][...] = total[:half]
            outs[2 * at + 1][...] = total[half:]
        else:
            outs[at][...] = total


def project(kernel, out_shape, place, *arrays):
    vmem = pl.BlockSpec(memory_space=pltpu.VMEM)
    rows, depth = arrays[0].shape
    outs = out_shape if isinstance(out_shape, list) else [out_shape]
    size = sum(math.prod(out.shape) for out in outs)
    return pl.pallas_call(
        kernel,
        out_shape=out_shape,
        in_specs=[pl.BlockSpec(memory_space=pltpu.SMEM)] + [vmem] * len(arrays),
        out_specs=[vmem] * len(outs) if isinstance(out_shape, list) else vmem,
        compiler_params=pltpu.CompilerParams(vmem_limit_bytes=20 * MIB),
        cost_estimate=pl.CostEstimate(
            flops=2 * size * depth, bytes_accessed=4 * MIB, transcendentals=0
        ),
    )(place, *arrays)


def project_other(place, mine, w_out, turns, width):
    shape = jax.ShapeDtypeStruct((len(turns), mine.shape[0], width), jnp.bfloat16)
    return project(functools.partial(project_other_kernel, turns), shape, place, mine, w_out)


def project_own(place, mine, w_out, turns, came, first, split=False):
    parts = 2 if split else 1
    shape = jax.ShapeDtypeStruct((mine.shape[0] // parts, came.shape[2]), jnp.bfloat16)
    kernel = functools.partial(project_own_kernel, turns, first, split)
    return project(kernel, [shape] * (parts * len(turns)), place, mine, w_out, came)


def merge_kernel(up, down, top, low, up_out, down_out):
    half = top.shape[0]
    up_out[:half] = (up[:half].astype(jnp.float32) + top[...]).astype(jnp.bfloat16)
    up_out[half:] = up[half:]
    down_out[:half] = down[:half]
    down_out[half:] = (down[half:].astype(jnp.float32) + low[...]).astype(jnp.bfloat16)


def merge(up, down, top, low):
    vmem = pl.BlockSpec(memory_space=pltpu.VMEM)
    return pl.pallas_call(
        merge_kernel,
        out_shape=[jax.ShapeDtypeStruct(up.shape, up.dtype)] * 2,
        in_specs=[vmem] * 4,
        out_specs=[vmem] * 2,
        compiler_params=pltpu.CompilerParams(vmem_limit_bytes=8 * MIB),
        cost_estimate=pl.CostEstimate(flops=0, bytes_accessed=MIB, transcendentals=0),
    )(up, down, top, low)


def final_kernel(suffix, chunks, order, *refs):
    o_ref = refs[-1]
    for lo, at in chunks:
        terms = refs[at : at + 3]
        for n in range(terms[0].shape[0] // suffix):
            here = slice(n * suffix, (n + 1) * suffix)
            total = sum(term[here].astype(jnp.float32) for term in terms)
            o_ref[order[lo + n]] = total.astype(jnp.bfloat16)


def again_kernel(suffix, chunks, order, *refs):
    refs[-1][...] = refs[-2][...]
    final_kernel(suffix, chunks, order, *refs[:-2], refs[-1])


class Projection:
    def __init__(self, place, w_out, mine, width, *tokens):
        near = project_other(place, mine, w_out, (2,), width)
        near, *self.tokens = together(near, *tokens)
        self.near = swap_core(near)
        self.project = functools.partial(project_own, place, mine, w_out)
        top2, low2 = self.project((2,), self.near, 0, True)
        later, self.top2, self.low2 = together(mine, top2, low2)
        self.rest = swap_core(project_other(place, later, w_out, (1, 3, 0), width))

    def across(self):
        return send_y(self.top2, 1), send_y(self.low2, -1)

    def beside(self):
        return self.project((1, 3), self.rest, 0)

    def own(self):
        return self.project((0,), self.rest, 2)[0]


def shards(queries, prefix_kv, suffix_kv, candidate_prefix, w_out):
    count, suffix, width = queries.shape
    length = prefix_kv.shape[2]
    out_width = w_out.shape[1] // (2 * NY)
    chunk = count // 2
    order, codes, info = plan(candidate_prefix)

    vmem = pl.BlockSpec(memory_space=pltpu.VMEM)
    smem = pl.BlockSpec(memory_space=pltpu.SMEM)
    out_shape = jax.ShapeDtypeStruct((count, suffix, out_width), jnp.bfloat16)
    limit = pltpu.CompilerParams(vmem_limit_bytes=12 * MIB)

    gather = Gather(prefix_kv.reshape(2, length, HD))
    (order, codes, info), sources = gather.early(order, codes, info)

    (mine,) = attend(order, codes, info, queries, suffix_kv, sources, 0, chunk, length, False)
    gather.late()
    mine = gather.last(mine.reshape(chunk * suffix, width))
    one = Projection(info, w_out, mine, out_width)
    top2, low2 = one.across()
    up, down = one.beside()
    (up, down, top2, low2, order2), sources = gather.finish(up, down, top2, low2, order)
    up, down = merge(up, down, top2, low2)
    up, down = send_y(up, 1), send_y(down, -1)

    mine, again = attend(
        order2, codes, info, queries, suffix_kv, sources, chunk, chunk, length, True
    )
    two = Projection(info, w_out, mine.reshape(chunk * suffix, width), out_width, up, down)
    up, down = two.tokens
    terms = [one.own(), up, down]
    top2, low2 = two.across()
    up, down = two.beside()
    up, down = merge(up, down, top2, low2)
    terms += [two.own(), send_y(up, 1), send_y(down, -1)]
    out = pl.pallas_call(
        functools.partial(final_kernel, suffix, [(0, 0), (chunk, 3)]),
        out_shape=out_shape,
        in_specs=[smem] + [vmem] * 6,
        out_specs=vmem,
        compiler_params=limit,
    )(order, *terms)

    def redo(state):
        left, out, again = state
        mine = again.reshape(chunk * suffix, width)
        extra = Projection(info, w_out, mine, out_width)
        top2, low2 = extra.across()
        up, down = merge(*extra.beside(), top2, low2)
        terms = [extra.own(), send_y(up, 1), send_y(down, -1)]
        out = pl.pallas_call(
            functools.partial(again_kernel, suffix, [(0, 0)]),
            out_shape=out_shape,
            in_specs=[smem] + [vmem] * 4,
            out_specs=vmem,
            compiler_params=limit,
        )(order, *terms, out)
        again, out = together(again, out)
        return left - 1, out, again

    left = (info[2] < chunk).astype(jnp.int32)
    return lax.while_loop(lambda state: state[0] > 0, redo, (left, out, again))[1]


def solution(mesh):
    in_specs = (
        P("cache", None, "tensor"),
        P(None, "cache", None, "tensor"),
        P(None, "cache", None, "tensor"),
        P("cache", None),
        P("tensor", None),
    )
    out_specs = P("cache", None, "tensor")
    return jax.shard_map(shards, mesh=mesh, in_specs=in_specs, out_specs=out_specs, check_vma=False)
```

```python
import functools
import math

import jax
import jax.numpy as jnp
from jax import lax
from jax.experimental import pallas as pl
from jax.experimental.pallas import tpu as pltpu
from jax.sharding import PartitionSpec as P

H = 64
KVH = 8
HD = 128
GROUP = H // KVH
NX = 4
NZ = 8
NY = 4
LOG2E = 1.4426950408889634
MIB = 1024 * 1024


def send_cache(value, along_z):
    pairs = []
    for x in range(NX):
        for z in range(NZ):
            for t in range(2 * NY):
                step = -1 if t % 2 else 1
                to_x, to_z = (x, (z + step) % NZ) if along_z else ((x + step) % NX, z)
                pairs.append(((x * NZ + z) * 2 * NY + t, (to_x * NZ + to_z) * 2 * NY + t))
    return lax.ppermute(value, ("cache", "tensor"), pairs)


def send_y(value, step):
    pairs = [(2 * y + c, 2 * ((y + step) % NY) + c) for y in range(NY) for c in range(2)]
    return lax.ppermute(value, "tensor", pairs)


def swap_core(value):
    return lax.ppermute(value, "tensor", [(t, t ^ 1) for t in range(2 * NY)])


def together(*values):
    return lax.optimization_barrier(values)


def pack_kernel(places, n_arrays, *refs):
    o_ref = refs[n_arrays]
    for index, (which, at) in places:
        o_ref[index] = refs[which][at]


def pack(parts):
    arrays = []
    places = []
    for i, row in enumerate(parts):
        for j, (array, at) in enumerate(row):
            which = next((n for n, a in enumerate(arrays) if a is array), len(arrays))
            if which == len(arrays):
                arrays.append(array)
            places.append(((i, j), (which, at)))
    block = arrays[0].shape[-2:]
    vmem = pl.BlockSpec(memory_space=pltpu.VMEM)
    return pl.pallas_call(
        functools.partial(pack_kernel, places, len(arrays)),
        out_shape=jax.ShapeDtypeStruct((len(parts), len(parts[0])) + block, jnp.bfloat16),
        in_specs=[vmem] * len(arrays),
        out_specs=vmem,
        compiler_params=pltpu.CompilerParams(vmem_limit_bytes=6 * MIB),
        cost_estimate=pl.CostEstimate(flops=0, bytes_accessed=MIB, transcendentals=0),
    )(*arrays)


class Gather:
    def __init__(self, block):
        self.block = block
        self.sources = {}

    def part(self, array, at, kv, dz, dx):
        code = (dz % NZ) * NX + dx % NX
        self.sources.setdefault(code, []).append((array, at, kv))

    def whole(self, array, at, dz, dx):
        for kv in range(2):
            self.part(array, at + (kv,), kv, dz, dx)

    def early(self, *tokens):
        block = self.block
        other = swap_core(block)
        both = pack([[(block, 0), (block, 1)], [(other, 0), (other, 1)]])
        x1, z1 = send_cache(both, False), send_cache(both, True)
        x1, z1, *tokens = together(x1, z1, *tokens)
        x1m, z1m = swap_core(x1), swap_core(z1)
        x2, z2 = send_cache(x1, False), send_cache(z1, True)
        x2, z2, x1m, z1m = together(x2, z2, x1m, z1m)
        values = pack(
            [
                [(x1, (0, 1)), (x1m, (1, 1)), (x2, (0, 1))],
                [(x1, (1, 1)), (x1m, (0, 1)), (x2, (1, 1))],
            ]
        )
        z2m = swap_core(z2)
        near = pack(
            [
                [(z1, (0, 0)), (z1m, (1, 0)), (z2, (0, 0)), (z2m, (1, 0))],
                [(z1, (1, 0)), (z1m, (0, 0)), (z2, (1, 0)), (z2m, (0, 0))],
            ]
        )
        v1, n1 = send_cache(values, True), send_cache(near, False)
        z3 = send_cache(z2, True)
        v1, n1, z3 = together(v1, n1, z3)
        z3m, n1m, v1m = swap_core(z3), swap_core(n1[1]), swap_core(v1[1])
        z4, n2, v2 = send_cache(z3[0], True), send_cache(n1[0], False), send_cache(v1, True)
        z4, n2, v2, z3m, n1m, v1m = together(z4, n2, v2, z3m, n1m, v1m)
        v2m = swap_core(v2[1])

        self.whole(block, (), 0, 0)
        self.whole(x1, (0,), 0, 1)
        self.whole(x1m, (1,), 0, -1)
        self.whole(x2, (0,), 0, 2)
        for step, mine, mate in ((1, z1, z1m), (2, z2, z2m), (3, z3, z3m)):
            self.whole(mine, (0,), step, 0)
            self.whole(mate, (1,), -step, 0)
        self.whole(z4, (), 4, 0)
        for step, mine, mate in ((1, v1, v1m), (2, v2, v2m)):
            self.values(mine, mate, step)
        for at, dz in enumerate((1, -1, 2, -2)):
            self.part(n1, (0, at), 0, dz, 1)
            self.part(n1m, (at,), 0, -dz, -1)
            self.part(n2, (at,), 0, dz, 2)
        self.left = v2, z3, z3m, z4
        return tokens, {code: list(parts) for code, parts in self.sources.items()}

    def values(self, mine, mate, step):
        for at, dx in enumerate((1, -1, 2)):
            self.part(mine, (0, at), 1, step, dx)
            self.part(mate, (at,), 1, -step, -dx)

    def late(self):
        v2, z3, z3m, z4 = self.left
        key_z4m = swap_core(z4[0:1])
        distant = pack(
            [
                [(z3, (0, 0)), (z3m, (1, 0)), (z4, 0)],
                [(z3, (1, 0)), (z3m, (0, 0)), (key_z4m, 0)],
            ]
        )
        self.hop = send_cache(v2, True), send_cache(distant, False)

    def last(self, token):
        token, v3, f1 = together(token, *self.hop)
        v4, f2 = send_cache(v3[0], True), send_cache(f1[0], False)
        self.final = v3, f1, v4, f2
        return token

    def finish(self, *tokens):
        count = len(tokens)
        done = together(*tokens, *self.final)
        v3, f1, v4, f2 = done[count:]
        third = range(3)
        rest = swap_core(pack([[(v3, (1, at)) for at in third], [(f1, (1, at)) for at in third]]))
        for at, dx in enumerate((1, -1, 2)):
            self.part(v3, (0, at), 1, 3, dx)
            self.part(rest, (0, at), 1, -3, -dx)
            self.part(v4, (at,), 1, 4, dx)
        for at, dz in enumerate((3, -3, 4)):
            self.part(f1, (0, at), 0, dz, 1)
            self.part(rest, (1, at), 0, -dz, -1)
            self.part(f2, (at,), 0, dz, 2)
        return done[:count], self.sources


LAST = (((1,), (1,)), ((), ()))
INNER = (((1,), (0,)), ((), ()))


def beside_ones(values):
    return jnp.concatenate([values, jnp.ones_like(values)], axis=1)


def plan_kernel(ids, order, codes, info):
    me = lax.axis_index("cache")
    t = lax.axis_index("tensor")
    count = ids.shape[0]
    info[0] = t // 2
    info[1] = t % 2

    def is_early(code):
        dz = code // NX
        return (code % NX == 0) | (dz <= 2) | (dz >= NZ - 2)

    def first(n, at):
        passage = ids[n]
        dz = (passage % NZ - me % NZ + NZ) % NZ
        dx = (passage // NZ - me // NZ + NX) % NX
        dz = jnp.where(t % 2 == 0, (NZ - dz) % NZ, dz)
        dx = jnp.where(t % 2 == 0, (NX - dx) % NX, dx)
        code = dz * NX + dx
        codes[n] = code
        order[at] = n
        return at + is_early(code).astype(jnp.int32)

    early = lax.fori_loop(0, count, first, jnp.int32(0))
    info[2] = early

    def second(n, at):
        late = jnp.logical_not(is_early(codes[n]))

        @pl.when(late)
        def _():
            order[at] = n

        return at + late.astype(jnp.int32)

    lax.fori_loop(0, count, second, early)


def plan(candidate_prefix):
    count = candidate_prefix.shape[0]
    smem = pl.BlockSpec(memory_space=pltpu.SMEM)
    return pl.pallas_call(
        plan_kernel,
        out_shape=[jax.ShapeDtypeStruct((n,), jnp.int32) for n in (count, count, 3)],
        in_specs=[smem],
        out_specs=[smem] * 3,
        compiler_params=pltpu.CompilerParams(vmem_limit_bytes=MIB),
        cost_estimate=pl.CostEstimate(flops=1000, bytes_accessed=1000, transcendentals=0),
    )(candidate_prefix.reshape(count))


def attention_kernel(sources, n_arrays, lo, count, batch, order, codes, info, q_ref, s_ref, *rest):
    arrays = rest[:n_arrays]
    *outs, cache = rest[n_arrays:]
    suffix = q_ref.shape[1]
    length = cache.shape[2]
    rows = GROUP * suffix
    factor = LOG2E / math.sqrt(HD)
    token = lax.broadcasted_iota(jnp.int32, (rows, HD), 0) % suffix
    causal = lax.broadcasted_iota(jnp.int32, (rows, HD), 1) <= token
    blank = jnp.zeros((HD - suffix, HD), jnp.bfloat16)

    def fetch(first, batch):
        @pl.loop(0, batch)
        def _(i):
            code = codes[order[first + i]]
            for dx in range(NX):

                @pl.when(code % NX == dx)
                def _(dx=dx):
                    for dz in range(NZ):
                        parts = sources.get(dz * NX + dx)
                        if parts is None:
                            continue

                        @pl.when(code // NX == dz)
                        def _(parts=parts):
                            for which, at, kv in parts:

                                @pl.loop(0, length // HD)
                                def _(r, which=which, at=at, kv=kv):
                                    here = pl.ds(pl.multiple_of(r * HD, HD), HD)
                                    index = at if isinstance(at, tuple) else (at,)
                                    cache[i, kv, here] = arrays[which][(*index, here)]

    def attend_batch(first, at, out, batch):
        fetch(first, batch)
        scores = []
        for i in range(batch):
            n = order[first + i]
            q = jnp.concatenate([q_ref[n, :, g * HD : (g + 1) * HD] for g in range(GROUP)], axis=0)
            far = lax.dot_general(q, cache[i, 0], LAST, preferred_element_type=jnp.float32)
            keys = jnp.concatenate([s_ref[0, n], blank], axis=0)
            near = lax.dot_general(q, keys, LAST, preferred_element_type=jnp.float32)
            near = jnp.where(causal, near, -jnp.inf)
            scores.append([far[:, j : j + HD] for j in range(0, far.shape[1], HD)] + [near])
        weights = []
        for tiles in scores:
            top = jnp.max(functools.reduce(jnp.maximum, tiles), axis=1, keepdims=True)
            weights.append([jnp.exp2((s - top) * factor).astype(jnp.bfloat16) for s in tiles])
        for i in range(batch):
            n = order[first + i]
            far = jnp.concatenate(weights[i][:-1], axis=1)
            near = weights[i][-1][:, :suffix]
            summed = lax.dot_general(
                far, beside_ones(cache[i, 1]), INNER, preferred_element_type=jnp.float32
            ) + lax.dot_general(
                near, beside_ones(s_ref[1, n]), INNER, preferred_element_type=jnp.float32
            )
            result = (summed[:, :HD] / summed[:, HD:]).astype(jnp.bfloat16)
            for g in range(GROUP):
                out[at + i, :, g * HD : (g + 1) * HD] = result[g * suffix : (g + 1) * suffix]

    @pl.loop(0, count // batch)
    def _(step):
        attend_batch(lo + step * batch, step * batch, outs[0], batch)

    if len(outs) > 1:
        @pl.loop(0, jnp.where(info[2] < lo, count, 0))
        def _(step):
            attend_batch(step, step, outs[1], 1)


def attend(order, codes, info, queries, suffix_kv, sources, lo, count, length, again):
    arrays = []
    places = {}
    for code, parts in sources.items():
        for array, at, kv in parts:
            which = next((n for n, a in enumerate(arrays) if a is array), len(arrays))
            if which == len(arrays):
                arrays.append(array)
            places.setdefault(code, []).append((which, at, kv))
    _, suffix, width = queries.shape
    batch = 4
    vmem = pl.BlockSpec(memory_space=pltpu.VMEM)
    smem = pl.BlockSpec(memory_space=pltpu.SMEM)
    shape = jax.ShapeDtypeStruct((count, suffix, width), jnp.bfloat16)
    outs = 2 if again else 1
    return pl.pallas_call(
        functools.partial(attention_kernel, places, len(arrays), lo, count, batch),
        out_shape=[shape] * outs,
        in_specs=[smem] * 3 + [vmem] * (2 + len(arrays)),
        out_specs=[vmem] * outs,
        scratch_shapes=[pltpu.VMEM((batch, 2, length, HD), jnp.bfloat16)],
        compiler_params=pltpu.CompilerParams(vmem_limit_bytes=28 * MIB),
        cost_estimate=pl.CostEstimate(
            flops=4 * count * suffix * width * length,
            bytes_accessed=8 * MIB,
            transcendentals=count * suffix * GROUP * length,
        ),
    )(order, codes, info, queries, suffix_kv, *arrays)


def columns_of(place, turn, other, width):
    core = 1 - place[1] if other else place[1]
    return pl.multiple_of((2 * lax.rem(place[0] + turn, NY) + core) * width, width)


def project_other_kernel(turns, place, a_ref, w_ref, o_ref):
    width = o_ref.shape[2]
    for at, turn in enumerate(turns):
        column = columns_of(place, turn, True, width)
        total = jnp.dot(
            a_ref[...], w_ref[:, pl.ds(column, width)], preferred_element_type=jnp.float32
        )
        o_ref[at] = total.astype(jnp.bfloat16)


def project_own_kernel(turns, first, split, place, a_ref, w_ref, came_ref, *outs):
    width = came_ref.shape[2]
    half = a_ref.shape[0] // 2
    for at, turn in enumerate(turns):
        column = columns_of(place, turn, False, width)
        total = jnp.dot(
            a_ref[...], w_ref[:, pl.ds(column, width)], preferred_element_type=jnp.float32
        )
        total = (total + came_ref[first + at].astype(jnp.float32)).astype(jnp.bfloat16)
        if split:
            outs[2 * at][...] = total[:half]
            outs[2 * at + 1][...] = total[half:]
        else:
            outs[at][...] = total


def project(kernel, out_shape, place, *arrays):
    vmem = pl.BlockSpec(memory_space=pltpu.VMEM)
    rows, depth = arrays[0].shape
    outs = out_shape if isinstance(out_shape, list) else [out_shape]
    size = sum(math.prod(out.shape) for out in outs)
    return pl.pallas_call(
        kernel,
        out_shape=out_shape,
        in_specs=[pl.BlockSpec(memory_space=pltpu.SMEM)] + [vmem] * len(arrays),
        out_specs=[vmem] * len(outs) if isinstance(out_shape, list) else vmem,
        compiler_params=pltpu.CompilerParams(vmem_limit_bytes=20 * MIB),
        cost_estimate=pl.CostEstimate(
            flops=2 * size * depth, bytes_accessed=4 * MIB, transcendentals=0
        ),
    )(place, *arrays)


def project_other(place, mine, w_out, turns, width):
    shape = jax.ShapeDtypeStruct((len(turns), mine.shape[0], width), jnp.bfloat16)
    return project(functools.partial(project_other_kernel, turns), shape, place, mine, w_out)


def project_own(place, mine, w_out, turns, came, first, split=False):
    parts = 2 if split else 1
    shape = jax.ShapeDtypeStruct((mine.shape[0] // parts, came.shape[2]), jnp.bfloat16)
    kernel = functools.partial(project_own_kernel, turns, first, split)
    return project(kernel, [shape] * (parts * len(turns)), place, mine, w_out, came)


def merge_kernel(up, down, top, low, up_out, down_out):
    half = top.shape[0]
    up_out[:half] = (up[:half].astype(jnp.float32) + top[...]).astype(jnp.bfloat16)
    up_out[half:] = up[half:]
    down_out[:half] = down[:half]
    down_out[half:] = (down[half:].astype(jnp.float32) + low[...]).astype(jnp.bfloat16)


def merge(up, down, top, low):
    vmem = pl.BlockSpec(memory_space=pltpu.VMEM)
    return pl.pallas_call(
        merge_kernel,
        out_shape=[jax.ShapeDtypeStruct(up.shape, up.dtype)] * 2,
        in_specs=[vmem] * 4,
        out_specs=[vmem] * 2,
        compiler_params=pltpu.CompilerParams(vmem_limit_bytes=8 * MIB),
        cost_estimate=pl.CostEstimate(flops=0, bytes_accessed=MIB, transcendentals=0),
    )(up, down, top, low)


def final_kernel(suffix, chunks, order, *refs):
    o_ref = refs[-1]
    for lo, at in chunks:
        terms = refs[at : at + 3]

        @pl.loop(0, terms[0].shape[0] // suffix)
        def _(n, lo=lo, terms=terms):
            here = pl.ds(pl.multiple_of(n * suffix, suffix), suffix)
            total = sum(term[here].astype(jnp.float32) for term in terms)
            o_ref[order[lo + n]] = total.astype(jnp.bfloat16)


def again_kernel(suffix, chunks, order, *refs):
    refs[-1][...] = refs[-2][...]
    final_kernel(suffix, chunks, order, *refs[:-2], refs[-1])


class Projection:
    def __init__(self, place, w_out, mine, width, *tokens):
        near = project_other(place, mine, w_out, (2,), width)
        near, *self.tokens = together(near, *tokens)
        self.near = swap_core(near)
        self.project = functools.partial(project_own, place, mine, w_out)
        top2, low2 = self.project((2,), self.near, 0, True)
        later, self.top2, self.low2 = together(mine, top2, low2)
        self.rest = swap_core(project_other(place, later, w_out, (1, 3, 0), width))

    def across(self):
        return send_y(self.top2, 1), send_y(self.low2, -1)

    def beside(self):
        return self.project((1, 3), self.rest, 0)

    def own(self):
        return self.project((0,), self.rest, 2)[0]


def project_again(place, w_out, mine, width):
    def share(turn, other):
        core = 1 - place[1] if other else place[1]
        column = (2 * ((place[0] + turn) % NY) + core) * width
        block = lax.dynamic_slice_in_dim(w_out, column, width, axis=1)
        return jnp.dot(mine, block, preferred_element_type=jnp.float32)

    def total(turn):
        came = swap_core(share(turn, True).astype(jnp.bfloat16))
        return (share(turn, False) + came.astype(jnp.float32)).astype(jnp.bfloat16)

    half = mine.shape[0] // 2
    across = total(2)
    top2, low2 = send_y(across[:half], 1), send_y(across[half:], -1)
    up, down = total(1), total(3)
    up = jnp.concatenate([added(up[:half], top2), up[half:]], axis=0)
    down = jnp.concatenate([down[:half], added(down[half:], low2)], axis=0)
    return [total(0), send_y(up, 1), send_y(down, -1)]


def added(*terms):
    return sum(t.astype(jnp.float32) for t in terms).astype(jnp.bfloat16)


def shards(queries, prefix_kv, suffix_kv, candidate_prefix, w_out):
    count, suffix, width = queries.shape
    length = prefix_kv.shape[2]
    out_width = w_out.shape[1] // (2 * NY)
    chunk = count // 2
    order, codes, info = plan(candidate_prefix)

    vmem = pl.BlockSpec(memory_space=pltpu.VMEM)
    smem = pl.BlockSpec(memory_space=pltpu.SMEM)
    out_shape = jax.ShapeDtypeStruct((count, suffix, out_width), jnp.bfloat16)
    limit = pltpu.CompilerParams(vmem_limit_bytes=12 * MIB)

    gather = Gather(prefix_kv.reshape(2, length, HD))
    (order, codes, info), sources = gather.early(order, codes, info)

    (mine,) = attend(order, codes, info, queries, suffix_kv, sources, 0, chunk, length, False)
    gather.late()
    mine = gather.last(mine.reshape(chunk * suffix, width))
    one = Projection(info, w_out, mine, out_width)
    top2, low2 = one.across()
    up, down = one.beside()
    (up, down, top2, low2, order2), sources = gather.finish(up, down, top2, low2, order)
    up, down = merge(up, down, top2, low2)
    up, down = send_y(up, 1), send_y(down, -1)

    mine, again = attend(
        order2, codes, info, queries, suffix_kv, sources, chunk, chunk, length, True
    )
    two = Projection(info, w_out, mine.reshape(chunk * suffix, width), out_width, up, down)
    up, down = two.tokens
    terms = [one.own(), up, down]
    top2, low2 = two.across()
    up, down = two.beside()
    up, down = merge(up, down, top2, low2)
    terms += [two.own(), send_y(up, 1), send_y(down, -1)]
    out = pl.pallas_call(
        functools.partial(final_kernel, suffix, [(0, 0), (chunk, 3)]),
        out_shape=out_shape,
        in_specs=[smem] + [vmem] * 6,
        out_specs=vmem,
        compiler_params=limit,
    )(order, *terms)

    def redo(state):
        left, out, again = state
        mine, weights, here = together(again, w_out, info)
        terms = project_again(here, weights, mine.reshape(chunk * suffix, width), out_width)
        out = pl.pallas_call(
            functools.partial(again_kernel, suffix, [(0, 0)]),
            out_shape=out_shape,
            in_specs=[smem] + [vmem] * 4,
            out_specs=vmem,
            compiler_params=limit,
        )(order, *terms, out)
        again, out = together(again, out)
        return left - 1, out, again

    left = (info[2] < chunk).astype(jnp.int32)
    return lax.while_loop(lambda state: state[0] > 0, redo, (left, out, again))[1]


def solution(mesh):
    in_specs = (
        P("cache", None, "tensor"),
        P(None, "cache", None, "tensor"),
        P(None, "cache", None, "tensor"),
        P("cache", None),
        P("tensor", None),
    )
    out_specs = P("cache", None, "tensor")
    return jax.shard_map(shards, mesh=mesh, in_specs=in_specs, out_specs=out_specs, check_vma=False)
```

```python
import functools
import math

import jax
import jax.numpy as jnp
from jax import lax
from jax.experimental import pallas as pl
from jax.experimental.pallas import tpu as pltpu
from jax.sharding import PartitionSpec as P

H = 64
KVH = 8
HD = 128
GROUP = H // KVH
NX = 4
NZ = 8
NY = 4
LATE = 9
LOG2E = 1.4426950408889634
MIB = 1024 * 1024


def send_cache(value, along_z):
    pairs = []
    for x in range(NX):
        for z in range(NZ):
            for t in range(2 * NY):
                step = -1 if t % 2 else 1
                to_x, to_z = (x, (z + step) % NZ) if along_z else ((x + step) % NX, z)
                pairs.append(((x * NZ + z) * 2 * NY + t, (to_x * NZ + to_z) * 2 * NY + t))
    return lax.ppermute(value, ("cache", "tensor"), pairs)


def send_y(value, step):
    pairs = [(2 * y + c, 2 * ((y + step) % NY) + c) for y in range(NY) for c in range(2)]
    return lax.ppermute(value, "tensor", pairs)


def swap_core(value):
    return lax.ppermute(value, "tensor", [(t, t ^ 1) for t in range(2 * NY)])


def together(*values):
    return lax.optimization_barrier(values)


def pack_kernel(places, n_arrays, *refs):
    o_ref = refs[n_arrays]
    for index, (which, at) in places:
        o_ref[index] = refs[which][at]


def pack(parts):
    arrays = []
    places = []
    for i, row in enumerate(parts):
        for j, (array, at) in enumerate(row):
            which = next((n for n, a in enumerate(arrays) if a is array), len(arrays))
            if which == len(arrays):
                arrays.append(array)
            places.append(((i, j), (which, at)))
    block = arrays[0].shape[-2:]
    vmem = pl.BlockSpec(memory_space=pltpu.VMEM)
    return pl.pallas_call(
        functools.partial(pack_kernel, places, len(arrays)),
        out_shape=jax.ShapeDtypeStruct((len(parts), len(parts[0])) + block, jnp.bfloat16),
        in_specs=[vmem] * len(arrays),
        out_specs=vmem,
        compiler_params=pltpu.CompilerParams(vmem_limit_bytes=6 * MIB),
        cost_estimate=pl.CostEstimate(flops=0, bytes_accessed=MIB, transcendentals=0),
    )(*arrays)


class Gather:
    def __init__(self, block):
        self.block = block
        self.sources = {}

    def part(self, array, at, kv, dz, dx):
        code = (dz % NZ) * NX + dx % NX
        self.sources.setdefault(code, []).append((array, at, kv))

    def whole(self, array, at, dz, dx):
        for kv in range(2):
            self.part(array, at + (kv,), kv, dz, dx)

    def early(self, *tokens):
        block = self.block
        other = swap_core(block)
        both = pack([[(block, 0), (block, 1)], [(other, 0), (other, 1)]])
        x1, z1 = send_cache(both, False), send_cache(both, True)
        x1, z1, *tokens = together(x1, z1, *tokens)
        x1m, z1m = swap_core(x1), swap_core(z1)
        x2, z2 = send_cache(x1, False), send_cache(z1, True)
        x2, z2, x1m, z1m = together(x2, z2, x1m, z1m)
        values = pack(
            [
                [(x1, (0, 1)), (x1m, (1, 1)), (x2, (0, 1))],
                [(x1, (1, 1)), (x1m, (0, 1)), (x2, (1, 1))],
            ]
        )
        z2m = swap_core(z2)
        near = pack(
            [
                [(z1, (0, 0)), (z1m, (1, 0)), (z2, (0, 0)), (z2m, (1, 0))],
                [(z1, (1, 0)), (z1m, (0, 0)), (z2, (1, 0)), (z2m, (0, 0))],
            ]
        )
        v1, n1 = send_cache(values, True), send_cache(near, False)
        z3 = send_cache(z2, True)
        v1, n1, z3 = together(v1, n1, z3)
        z3m, n1m, v1m = swap_core(z3), swap_core(n1[1]), swap_core(v1[1])
        z4, n2, v2 = send_cache(z3[0], True), send_cache(n1[0], False), send_cache(v1, True)
        z4, n2, v2, z3m, n1m, v1m = together(z4, n2, v2, z3m, n1m, v1m)
        v2m = swap_core(v2[1])

        self.whole(block, (), 0, 0)
        self.whole(x1, (0,), 0, 1)
        self.whole(x1m, (1,), 0, -1)
        self.whole(x2, (0,), 0, 2)
        for step, mine, mate in ((1, z1, z1m), (2, z2, z2m), (3, z3, z3m)):
            self.whole(mine, (0,), step, 0)
            self.whole(mate, (1,), -step, 0)
        self.whole(z4, (), 4, 0)
        for step, mine, mate in ((1, v1, v1m), (2, v2, v2m)):
            self.values(mine, mate, step)
        for at, dz in enumerate((1, -1, 2, -2)):
            self.part(n1, (0, at), 0, dz, 1)
            self.part(n1m, (at,), 0, -dz, -1)
            self.part(n2, (at,), 0, dz, 2)
        self.left = v2, z3, z3m, z4
        return tokens, {code: list(parts) for code, parts in self.sources.items()}

    def values(self, mine, mate, step):
        for at, dx in enumerate((1, -1, 2)):
            self.part(mine, (0, at), 1, step, dx)
            self.part(mate, (at,), 1, -step, -dx)

    def late(self):
        v2, z3, z3m, z4 = self.left
        key_z4m = swap_core(z4[0:1])
        distant = pack(
            [
                [(z3, (0, 0)), (z3m, (1, 0)), (z4, 0)],
                [(z3, (1, 0)), (z3m, (0, 0)), (key_z4m, 0)],
            ]
        )
        self.hop = send_cache(v2, True), send_cache(distant, False)

    def last(self, token):
        token, v3, f1 = together(token, *self.hop)
        v4, f2 = send_cache(v3[0], True), send_cache(f1[0], False)
        self.final = v3, f1, v4, f2
        return token

    def finish(self, *tokens):
        count = len(tokens)
        done = together(*tokens, *self.final)
        v3, f1, v4, f2 = done[count:]
        third = range(3)
        rest = swap_core(pack([[(v3, (1, at)) for at in third], [(f1, (1, at)) for at in third]]))
        for at, dx in enumerate((1, -1, 2)):
            self.part(v3, (0, at), 1, 3, dx)
            self.part(rest, (0, at), 1, -3, -dx)
            self.part(v4, (at,), 1, 4, dx)
        for at, dz in enumerate((3, -3, 4)):
            self.part(f1, (0, at), 0, dz, 1)
            self.part(rest, (1, at), 0, -dz, -1)
            self.part(f2, (at,), 0, dz, 2)
        return done[:count], self.sources


LAST = (((1,), (1,)), ((), ()))
INNER = (((1,), (0,)), ((), ()))


def beside_ones(values):
    return jnp.concatenate([values, jnp.ones_like(values)], axis=1)


def plan_kernel(ids, order, codes, info):
    me = lax.axis_index("cache")
    t = lax.axis_index("tensor")
    count = ids.shape[0]
    info[0] = t // 2
    info[1] = t % 2

    def is_early(code):
        dz = code // NX
        return (code % NX == 0) | (dz <= 2) | (dz >= NZ - 2)

    def first(n, at):
        passage = ids[n]
        dz = (passage % NZ - me % NZ + NZ) % NZ
        dx = (passage // NZ - me // NZ + NX) % NX
        dz = jnp.where(t % 2 == 0, (NZ - dz) % NZ, dz)
        dx = jnp.where(t % 2 == 0, (NX - dx) % NX, dx)
        code = dz * NX + dx
        codes[n] = code
        order[at] = n
        return at + is_early(code).astype(jnp.int32)

    early = lax.fori_loop(0, count, first, jnp.int32(0))

    def second(n, at):
        late = jnp.logical_not(is_early(codes[n]))

        @pl.when(late)
        def _():
            order[at] = n

        return at + late.astype(jnp.int32)

    lax.fori_loop(0, count, second, early)


def plan(candidate_prefix):
    count = candidate_prefix.shape[0]
    smem = pl.BlockSpec(memory_space=pltpu.SMEM)
    return pl.pallas_call(
        plan_kernel,
        out_shape=[jax.ShapeDtypeStruct((n,), jnp.int32) for n in (count, count, 2)],
        in_specs=[smem],
        out_specs=[smem] * 3,
        compiler_params=pltpu.CompilerParams(vmem_limit_bytes=MIB),
        cost_estimate=pl.CostEstimate(flops=1000, bytes_accessed=1000, transcendentals=0),
    )(candidate_prefix.reshape(count))


def attention_kernel(sources, n_arrays, lo, count, batch, order, codes, q_ref, s_ref, *rest):
    arrays = rest[:n_arrays]
    o_ref, cache = rest[n_arrays:]
    suffix = q_ref.shape[1]
    rows = GROUP * suffix
    factor = LOG2E / math.sqrt(HD)
    token = lax.broadcasted_iota(jnp.int32, (rows, HD), 0) % suffix
    causal = lax.broadcasted_iota(jnp.int32, (rows, HD), 1) <= token
    blank = jnp.zeros((HD - suffix, HD), jnp.bfloat16)

    def fetch(first):
        @pl.loop(0, batch)
        def _(i):
            code = codes[order[first + i]]
            for dx in range(NX):

                @pl.when(code % NX == dx)
                def _(dx=dx):
                    for dz in range(NZ):
                        parts = sources.get(dz * NX + dx)
                        if parts is None:
                            continue

                        @pl.when(code // NX == dz)
                        def _(parts=parts):
                            for which, at, kv in parts:
                                cache[i, kv] = arrays[which][at]

    def attend_batch(first, at):
        fetch(first)
        scores = []
        for i in range(batch):
            n = order[first + i]
            q = jnp.concatenate([q_ref[n, :, g * HD : (g + 1) * HD] for g in range(GROUP)], axis=0)
            far = lax.dot_general(q, cache[i, 0], LAST, preferred_element_type=jnp.float32)
            keys = jnp.concatenate([s_ref[0, n], blank], axis=0)
            near = lax.dot_general(q, keys, LAST, preferred_element_type=jnp.float32)
            near = jnp.where(causal, near, -jnp.inf)
            scores.append([far[:, j : j + HD] for j in range(0, far.shape[1], HD)] + [near])
        weights = []
        for tiles in scores:
            top = jnp.max(functools.reduce(jnp.maximum, tiles), axis=1, keepdims=True)
            weights.append([jnp.exp2((s - top) * factor).astype(jnp.bfloat16) for s in tiles])
        for i in range(batch):
            n = order[first + i]
            far = jnp.concatenate(weights[i][:-1], axis=1)
            near = weights[i][-1][:, :suffix]
            summed = lax.dot_general(
                far, beside_ones(cache[i, 1]), INNER, preferred_element_type=jnp.float32
            ) + lax.dot_general(
                near, beside_ones(s_ref[1, n]), INNER, preferred_element_type=jnp.float32
            )
            result = (summed[:, :HD] / summed[:, HD:]).astype(jnp.bfloat16)
            for g in range(GROUP):
                o_ref[at + i, :, g * HD : (g + 1) * HD] = result[g * suffix : (g + 1) * suffix]

    @pl.loop(0, -(-count // batch))
    def _(step):
        at = jnp.minimum(step * batch, count - batch)
        attend_batch(lo + at, at)


def attend(order, codes, queries, suffix_kv, sources, lo, count, length):
    arrays = []
    places = {}
    for code, parts in sources.items():
        for array, at, kv in parts:
            which = next((n for n, a in enumerate(arrays) if a is array), len(arrays))
            if which == len(arrays):
                arrays.append(array)
            places.setdefault(code, []).append((which, at, kv))
    _, suffix, width = queries.shape
    batch = 4
    vmem = pl.BlockSpec(memory_space=pltpu.VMEM)
    smem = pl.BlockSpec(memory_space=pltpu.SMEM)
    shape = jax.ShapeDtypeStruct((count, suffix, width), jnp.bfloat16)
    return pl.pallas_call(
        functools.partial(attention_kernel, places, len(arrays), lo, count, batch),
        out_shape=shape,
        in_specs=[smem] * 2 + [vmem] * (2 + len(arrays)),
        out_specs=vmem,
        scratch_shapes=[pltpu.VMEM((batch, 2, length, HD), jnp.bfloat16)],
        compiler_params=pltpu.CompilerParams(vmem_limit_bytes=28 * MIB),
        cost_estimate=pl.CostEstimate(
            flops=4 * count * suffix * width * length,
            bytes_accessed=8 * MIB,
            transcendentals=count * suffix * GROUP * length,
        ),
    )(order, codes, queries, suffix_kv, *arrays)


def columns_of(place, turn, other, width):
    core = 1 - place[1] if other else place[1]
    return pl.multiple_of((2 * lax.rem(place[0] + turn, NY) + core) * width, width)


def project_other_kernel(turns, place, a_ref, w_ref, o_ref):
    width = o_ref.shape[2]
    for at, turn in enumerate(turns):
        column = columns_of(place, turn, True, width)
        total = jnp.dot(
            a_ref[...], w_ref[:, pl.ds(column, width)], preferred_element_type=jnp.float32
        )
        o_ref[at] = total.astype(jnp.bfloat16)


def project_own_kernel(turns, first, split, place, a_ref, w_ref, came_ref, *outs):
    width = came_ref.shape[2]
    half = a_ref.shape[0] // 2
    for at, turn in enumerate(turns):
        column = columns_of(place, turn, False, width)
        total = jnp.dot(
            a_ref[...], w_ref[:, pl.ds(column, width)], preferred_element_type=jnp.float32
        )
        total = (total + came_ref[first + at].astype(jnp.float32)).astype(jnp.bfloat16)
        if split:
            outs[2 * at][...] = total[:half]
            outs[2 * at + 1][...] = total[half:]
        else:
            outs[at][...] = total


def project(kernel, out_shape, place, *arrays):
    vmem = pl.BlockSpec(memory_space=pltpu.VMEM)
    rows, depth = arrays[0].shape
    outs = out_shape if isinstance(out_shape, list) else [out_shape]
    size = sum(math.prod(out.shape) for out in outs)
    return pl.pallas_call(
        kernel,
        out_shape=out_shape,
        in_specs=[pl.BlockSpec(memory_space=pltpu.SMEM)] + [vmem] * len(arrays),
        out_specs=[vmem] * len(outs) if isinstance(out_shape, list) else vmem,
        compiler_params=pltpu.CompilerParams(vmem_limit_bytes=20 * MIB),
        cost_estimate=pl.CostEstimate(
            flops=2 * size * depth, bytes_accessed=4 * MIB, transcendentals=0
        ),
    )(place, *arrays)


def project_other(place, mine, w_out, turns, width):
    shape = jax.ShapeDtypeStruct((len(turns), mine.shape[0], width), jnp.bfloat16)
    return project(functools.partial(project_other_kernel, turns), shape, place, mine, w_out)


def project_own(place, mine, w_out, turns, came, first, split=False):
    parts = 2 if split else 1
    shape = jax.ShapeDtypeStruct((mine.shape[0] // parts, came.shape[2]), jnp.bfloat16)
    kernel = functools.partial(project_own_kernel, turns, first, split)
    return project(kernel, [shape] * (parts * len(turns)), place, mine, w_out, came)


def merge_kernel(up, down, top, low, up_out, down_out):
    half = top.shape[0]
    up_out[:half] = (up[:half].astype(jnp.float32) + top[...]).astype(jnp.bfloat16)
    up_out[half:] = up[half:]
    down_out[:half] = down[:half]
    down_out[half:] = (down[half:].astype(jnp.float32) + low[...]).astype(jnp.bfloat16)


def merge(up, down, top, low):
    vmem = pl.BlockSpec(memory_space=pltpu.VMEM)
    return pl.pallas_call(
        merge_kernel,
        out_shape=[jax.ShapeDtypeStruct(up.shape, up.dtype)] * 2,
        in_specs=[vmem] * 4,
        out_specs=[vmem] * 2,
        compiler_params=pltpu.CompilerParams(vmem_limit_bytes=8 * MIB),
        cost_estimate=pl.CostEstimate(flops=0, bytes_accessed=MIB, transcendentals=0),
    )(up, down, top, low)


def final_kernel(suffix, chunks, order, *refs):
    o_ref = refs[-1]
    for lo, at in chunks:
        terms = refs[at : at + 3]

        @pl.loop(0, terms[0].shape[0] // suffix)
        def _(n, lo=lo, terms=terms):
            here = pl.ds(pl.multiple_of(n * suffix, suffix), suffix)
            total = sum(term[here].astype(jnp.float32) for term in terms)
            o_ref[order[lo + n]] = total.astype(jnp.bfloat16)


class Projection:
    def __init__(self, place, w_out, mine, width, *tokens):
        near = project_other(place, mine, w_out, (2,), width)
        near, *self.tokens = together(near, *tokens)
        self.near = swap_core(near)
        self.project = functools.partial(project_own, place, mine, w_out)
        top2, low2 = self.project((2,), self.near, 0, True)
        later, self.top2, self.low2 = together(mine, top2, low2)
        self.rest = swap_core(project_other(place, later, w_out, (1, 3, 0), width))

    def across(self):
        return send_y(self.top2, 1), send_y(self.low2, -1)

    def beside(self):
        return self.project((1, 3), self.rest, 0)

    def own(self):
        return self.project((0,), self.rest, 2)[0]


def shards(queries, prefix_kv, suffix_kv, candidate_prefix, w_out):
    count, suffix, width = queries.shape
    length = prefix_kv.shape[2]
    out_width = w_out.shape[1] // (2 * NY)
    chunk = count - 2 * LATE
    others = count - chunk
    order, codes, info = plan(candidate_prefix)

    gather = Gather(prefix_kv.reshape(2, length, HD))
    (order, codes, info), sources = gather.early(order, codes, info)

    mine = attend(order, codes, queries, suffix_kv, sources, 0, chunk, length)
    gather.late()
    mine = gather.last(mine.reshape(chunk * suffix, width))
    one = Projection(info, w_out, mine, out_width)
    top2, low2 = one.across()
    up, down = one.beside()
    (up, down, top2, low2, order2), sources = gather.finish(up, down, top2, low2, order)
    up, down = merge(up, down, top2, low2)
    up, down = send_y(up, 1), send_y(down, -1)

    mine = attend(order2, codes, queries, suffix_kv, sources, chunk, others, length)
    two = Projection(info, w_out, mine.reshape(others * suffix, width), out_width, up, down)
    up, down = two.tokens
    terms = [one.own(), up, down]
    top2, low2 = two.across()
    up, down = two.beside()
    up, down = merge(up, down, top2, low2)
    terms += [two.own(), send_y(up, 1), send_y(down, -1)]
    return pl.pallas_call(
        functools.partial(final_kernel, suffix, [(0, 0), (chunk, 3)]),
        out_shape=jax.ShapeDtypeStruct((count, suffix, out_width), jnp.bfloat16),
        in_specs=[pl.BlockSpec(memory_space=pltpu.SMEM)]
        + [pl.BlockSpec(memory_space=pltpu.VMEM)] * 6,
        out_specs=pl.BlockSpec(memory_space=pltpu.VMEM),
        compiler_params=pltpu.CompilerParams(vmem_limit_bytes=12 * MIB),
    )(order, *terms)


def solution(mesh):
    in_specs = (
        P("cache", None, "tensor"),
        P(None, "cache", None, "tensor"),
        P(None, "cache", None, "tensor"),
        P("cache", None),
        P("tensor", None),
    )
    out_specs = P("cache", None, "tensor")
    return jax.shard_map(shards, mesh=mesh, in_specs=in_specs, out_specs=out_specs, check_vma=False)
```

```python
import functools
import math

import jax
import jax.numpy as jnp
from jax import lax
from jax.experimental import pallas as pl
from jax.experimental.pallas import tpu as pltpu
from jax.sharding import PartitionSpec as P

H = 64
KVH = 8
HD = 128
GROUP = H // KVH
NX = 4
NZ = 8
NY = 4
LATE = 9
LOG2E = 1.4426950408889634
MIB = 1024 * 1024


def send_cache(value, along_z):
    pairs = []
    for x in range(NX):
        for z in range(NZ):
            for t in range(2 * NY):
                step = -1 if t % 2 else 1
                to_x, to_z = (x, (z + step) % NZ) if along_z else ((x + step) % NX, z)
                pairs.append(((x * NZ + z) * 2 * NY + t, (to_x * NZ + to_z) * 2 * NY + t))
    return lax.ppermute(value, ("cache", "tensor"), pairs)


def send_y(value, step):
    pairs = [(2 * y + c, 2 * ((y + step) % NY) + c) for y in range(NY) for c in range(2)]
    return lax.ppermute(value, "tensor", pairs)


def swap_core(value):
    return lax.ppermute(value, "tensor", [(t, t ^ 1) for t in range(2 * NY)])


def together(*values):
    return lax.optimization_barrier(values)


def pack_kernel(places, n_arrays, *refs):
    o_ref = refs[n_arrays]
    for index, (which, at) in places:
        o_ref[index] = refs[which][at]


def pack(parts):
    arrays = []
    places = []
    for i, row in enumerate(parts):
        for j, (array, at) in enumerate(row):
            which = next((n for n, a in enumerate(arrays) if a is array), len(arrays))
            if which == len(arrays):
                arrays.append(array)
            places.append(((i, j), (which, at)))
    block = arrays[0].shape[-2:]
    vmem = pl.BlockSpec(memory_space=pltpu.VMEM)
    return pl.pallas_call(
        functools.partial(pack_kernel, places, len(arrays)),
        out_shape=jax.ShapeDtypeStruct((len(parts), len(parts[0])) + block, jnp.bfloat16),
        in_specs=[vmem] * len(arrays),
        out_specs=vmem,
        compiler_params=pltpu.CompilerParams(vmem_limit_bytes=6 * MIB),
        cost_estimate=pl.CostEstimate(flops=0, bytes_accessed=MIB, transcendentals=0),
    )(*arrays)


class Gather:
    def __init__(self, block):
        self.block = block
        self.sources = {}

    def part(self, array, at, kv, dz, dx):
        code = (dz % NZ) * NX + dx % NX
        self.sources.setdefault(code, []).append((array, at, kv))

    def whole(self, array, at, dz, dx):
        for kv in range(2):
            self.part(array, at + (kv,), kv, dz, dx)

    def early(self, *tokens):
        block = self.block
        other = swap_core(block)
        both = pack([[(block, 0), (block, 1)], [(other, 0), (other, 1)]])
        x1, z1 = send_cache(both, False), send_cache(both, True)
        x1, z1, *tokens = together(x1, z1, *tokens)
        x1m, z1m = swap_core(x1), swap_core(z1)
        x2, z2 = send_cache(x1, False), send_cache(z1, True)
        x2, z2, x1m, z1m = together(x2, z2, x1m, z1m)
        values = pack(
            [
                [(x1, (0, 1)), (x1m, (1, 1)), (x2, (0, 1))],
                [(x1, (1, 1)), (x1m, (0, 1)), (x2, (1, 1))],
            ]
        )
        z2m = swap_core(z2)
        near = pack(
            [
                [(z1, (0, 0)), (z1m, (1, 0)), (z2, (0, 0)), (z2m, (1, 0))],
                [(z1, (1, 0)), (z1m, (0, 0)), (z2, (1, 0)), (z2m, (0, 0))],
            ]
        )
        v1, n1 = send_cache(values, True), send_cache(near, False)
        z3 = send_cache(z2, True)
        v1, n1, z3 = together(v1, n1, z3)
        z3m, n1m, v1m = swap_core(z3), swap_core(n1[1]), swap_core(v1[1])
        z4, n2, v2 = send_cache(z3[0], True), send_cache(n1[0], False), send_cache(v1, True)
        z4, n2, v2, z3m, n1m, v1m = together(z4, n2, v2, z3m, n1m, v1m)
        v2m = swap_core(v2[1])

        self.whole(block, (), 0, 0)
        self.whole(x1, (0,), 0, 1)
        self.whole(x1m, (1,), 0, -1)
        self.whole(x2, (0,), 0, 2)
        for step, mine, mate in ((1, z1, z1m), (2, z2, z2m), (3, z3, z3m)):
            self.whole(mine, (0,), step, 0)
            self.whole(mate, (1,), -step, 0)
        self.whole(z4, (), 4, 0)
        for step, mine, mate in ((1, v1, v1m), (2, v2, v2m)):
            self.values(mine, mate, step)
        for at, dz in enumerate((1, -1, 2, -2)):
            self.part(n1, (0, at), 0, dz, 1)
            self.part(n1m, (at,), 0, -dz, -1)
            self.part(n2, (at,), 0, dz, 2)
        self.left = v2, z3, z3m, z4
        return tokens, {code: list(parts) for code, parts in self.sources.items()}

    def values(self, mine, mate, step):
        for at, dx in enumerate((1, -1, 2)):
            self.part(mine, (0, at), 1, step, dx)
            self.part(mate, (at,), 1, -step, -dx)

    def late(self):
        v2, z3, z3m, z4 = self.left
        key_z4m = swap_core(z4[0:1])
        distant = pack(
            [
                [(z3, (0, 0)), (z3m, (1, 0)), (z4, 0)],
                [(z3, (1, 0)), (z3m, (0, 0)), (key_z4m, 0)],
            ]
        )
        self.hop = send_cache(v2, True), send_cache(distant, False)

    def last(self, token):
        token, v3, f1 = together(token, *self.hop)
        v4, f2 = send_cache(v3[0], True), send_cache(f1[0], False)
        self.final = v3, f1, v4, f2
        return token

    def finish(self, *tokens):
        count = len(tokens)
        done = together(*tokens, *self.final)
        v3, f1, v4, f2 = done[count:]
        third = range(3)
        rest = swap_core(pack([[(v3, (1, at)) for at in third], [(f1, (1, at)) for at in third]]))
        for at, dx in enumerate((1, -1, 2)):
            self.part(v3, (0, at), 1, 3, dx)
            self.part(rest, (0, at), 1, -3, -dx)
            self.part(v4, (at,), 1, 4, dx)
        for at, dz in enumerate((3, -3, 4)):
            self.part(f1, (0, at), 0, dz, 1)
            self.part(rest, (1, at), 0, -dz, -1)
            self.part(f2, (at,), 0, dz, 2)
        return done[:count], self.sources


LAST = (((1,), (1,)), ((), ()))
INNER = (((1,), (0,)), ((), ()))


def beside_ones(values):
    return jnp.concatenate([values, jnp.ones_like(values)], axis=1)


def plan_kernel(ids, order, codes, info):
    me = lax.axis_index("cache")
    t = lax.axis_index("tensor")
    count = ids.shape[0]
    info[0] = t // 2
    info[1] = t % 2

    def is_early(code):
        dz = code // NX
        return (code % NX == 0) | (dz <= 2) | (dz >= NZ - 2)

    def first(n, at):
        passage = ids[n]
        dz = (passage % NZ - me % NZ + NZ) % NZ
        dx = (passage // NZ - me // NZ + NX) % NX
        dz = jnp.where(t % 2 == 0, (NZ - dz) % NZ, dz)
        dx = jnp.where(t % 2 == 0, (NX - dx) % NX, dx)
        code = dz * NX + dx
        codes[n] = code
        order[at] = n
        return at + is_early(code).astype(jnp.int32)

    early = lax.fori_loop(0, count, first, jnp.int32(0))

    def second(n, at):
        late = jnp.logical_not(is_early(codes[n]))

        @pl.when(late)
        def _():
            order[at] = n

        return at + late.astype(jnp.int32)

    lax.fori_loop(0, count, second, early)


def plan(candidate_prefix):
    count = candidate_prefix.shape[0]
    smem = pl.BlockSpec(memory_space=pltpu.SMEM)
    return pl.pallas_call(
        plan_kernel,
        out_shape=[jax.ShapeDtypeStruct((n,), jnp.int32) for n in (count, count, 2)],
        in_specs=[smem],
        out_specs=[smem] * 3,
        compiler_params=pltpu.CompilerParams(vmem_limit_bytes=MIB),
        cost_estimate=pl.CostEstimate(flops=1000, bytes_accessed=1000, transcendentals=0),
    )(candidate_prefix.reshape(count))


def attention_kernel(sources, n_arrays, lo, count, batch, order, codes, q_ref, s_ref, *rest):
    arrays = rest[:n_arrays]
    o_ref, cache = rest[n_arrays:]
    suffix = q_ref.shape[1]
    rows = GROUP * suffix
    factor = LOG2E / math.sqrt(HD)
    token = lax.broadcasted_iota(jnp.int32, (rows, HD), 0) % suffix
    causal = lax.broadcasted_iota(jnp.int32, (rows, HD), 1) <= token
    blank = jnp.zeros((HD - suffix, HD), jnp.bfloat16)

    def fetch(first):
        @pl.loop(0, batch)
        def _(i):
            code = codes[order[first + i]]
            for dx in range(NX):

                @pl.when(code % NX == dx)
                def _(dx=dx):
                    for dz in range(NZ):
                        parts = sources.get(dz * NX + dx)
                        if parts is None:
                            continue

                        @pl.when(code // NX == dz)
                        def _(parts=parts):
                            for which, at, kv in parts:
                                cache[i, kv] = arrays[which][at]

    def attend_batch(first, at):
        fetch(first)
        scores = []
        for i in range(batch):
            n = order[first + i]
            q = jnp.concatenate([q_ref[n, :, g * HD : (g + 1) * HD] for g in range(GROUP)], axis=0)
            far = lax.dot_general(q, cache[i, 0], LAST, preferred_element_type=jnp.float32)
            keys = jnp.concatenate([s_ref[0, n], blank], axis=0)
            near = lax.dot_general(q, keys, LAST, preferred_element_type=jnp.float32)
            near = jnp.where(causal, near, -jnp.inf)
            scores.append([far[:, j : j + HD] for j in range(0, far.shape[1], HD)] + [near])
        weights = []
        for tiles in scores:
            top = jnp.max(functools.reduce(jnp.maximum, tiles), axis=1, keepdims=True)
            weights.append([jnp.exp2((s - top) * factor).astype(jnp.bfloat16) for s in tiles])
        for i in range(batch):
            n = order[first + i]
            far = jnp.concatenate(weights[i][:-1], axis=1)
            near = weights[i][-1][:, :suffix]
            summed = lax.dot_general(
                far, beside_ones(cache[i, 1]), INNER, preferred_element_type=jnp.float32
            ) + lax.dot_general(
                near, beside_ones(s_ref[1, n]), INNER, preferred_element_type=jnp.float32
            )
            result = (summed[:, :HD] / summed[:, HD:]).astype(jnp.bfloat16)
            for g in range(GROUP):
                o_ref[at + i, :, g * HD : (g + 1) * HD] = result[g * suffix : (g + 1) * suffix]

    @pl.loop(0, -(-count // batch))
    def _(step):
        at = jnp.minimum(step * batch, count - batch)
        attend_batch(lo + at, at)


def attend(order, codes, queries, suffix_kv, sources, lo, count, length):
    arrays = []
    places = {}
    for code, parts in sources.items():
        for array, at, kv in parts:
            which = next((n for n, a in enumerate(arrays) if a is array), len(arrays))
            if which == len(arrays):
                arrays.append(array)
            places.setdefault(code, []).append((which, at, kv))
    _, suffix, width = queries.shape
    batch = 4
    vmem = pl.BlockSpec(memory_space=pltpu.VMEM)
    smem = pl.BlockSpec(memory_space=pltpu.SMEM)
    shape = jax.ShapeDtypeStruct((count, suffix, width), jnp.bfloat16)
    return pl.pallas_call(
        functools.partial(attention_kernel, places, len(arrays), lo, count, batch),
        out_shape=shape,
        in_specs=[smem] * 2 + [vmem] * (2 + len(arrays)),
        out_specs=vmem,
        scratch_shapes=[pltpu.VMEM((batch, 2, length, HD), jnp.bfloat16)],
        compiler_params=pltpu.CompilerParams(vmem_limit_bytes=28 * MIB),
        cost_estimate=pl.CostEstimate(
            flops=4 * count * suffix * width * length,
            bytes_accessed=8 * MIB,
            transcendentals=count * suffix * GROUP * length,
        ),
    )(order, codes, queries, suffix_kv, *arrays)


def columns_of(place, turn, other, width):
    core = 1 - place[1] if other else place[1]
    return pl.multiple_of((2 * lax.rem(place[0] + turn, NY) + core) * width, width)


def project_other_kernel(turns, place, a_ref, w_ref, o_ref):
    width = o_ref.shape[2]
    for at, turn in enumerate(turns):
        column = columns_of(place, turn, True, width)
        total = jnp.dot(
            a_ref[...], w_ref[:, pl.ds(column, width)], preferred_element_type=jnp.float32
        )
        o_ref[at] = total.astype(jnp.bfloat16)


def project_own_kernel(turns, first, split, place, a_ref, w_ref, came_ref, *outs):
    width = came_ref.shape[2]
    half = a_ref.shape[0] // 2
    for at, turn in enumerate(turns):
        column = columns_of(place, turn, False, width)
        total = jnp.dot(
            a_ref[...], w_ref[:, pl.ds(column, width)], preferred_element_type=jnp.float32
        )
        total = (total + came_ref[first + at].astype(jnp.float32)).astype(jnp.bfloat16)
        if split:
            outs[2 * at][...] = total[:half]
            outs[2 * at + 1][...] = total[half:]
        else:
            outs[at][...] = total


def project(kernel, out_shape, place, *arrays):
    vmem = pl.BlockSpec(memory_space=pltpu.VMEM)
    rows, depth = arrays[0].shape
    outs = out_shape if isinstance(out_shape, list) else [out_shape]
    size = sum(math.prod(out.shape) for out in outs)
    return pl.pallas_call(
        kernel,
        out_shape=out_shape,
        in_specs=[pl.BlockSpec(memory_space=pltpu.SMEM)] + [vmem] * len(arrays),
        out_specs=[vmem] * len(outs) if isinstance(out_shape, list) else vmem,
        compiler_params=pltpu.CompilerParams(vmem_limit_bytes=20 * MIB),
        cost_estimate=pl.CostEstimate(
            flops=2 * size * depth, bytes_accessed=4 * MIB, transcendentals=0
        ),
    )(place, *arrays)


def project_other(place, mine, w_out, turns, width):
    shape = jax.ShapeDtypeStruct((len(turns), mine.shape[0], width), jnp.bfloat16)
    return project(functools.partial(project_other_kernel, turns), shape, place, mine, w_out)


def project_own(place, mine, w_out, turns, came, first, split=False):
    parts = 2 if split else 1
    shape = jax.ShapeDtypeStruct((mine.shape[0] // parts, came.shape[2]), jnp.bfloat16)
    kernel = functools.partial(project_own_kernel, turns, first, split)
    return project(kernel, [shape] * (parts * len(turns)), place, mine, w_out, came)


def merge_kernel(up, down, top, low, up_out, down_out):
    half = top.shape[0]
    up_out[:half] = (up[:half].astype(jnp.float32) + top[...]).astype(jnp.bfloat16)
    up_out[half:] = up[half:]
    down_out[:half] = down[:half]
    down_out[half:] = (down[half:].astype(jnp.float32) + low[...]).astype(jnp.bfloat16)


def merge(up, down, top, low):
    vmem = pl.BlockSpec(memory_space=pltpu.VMEM)
    return pl.pallas_call(
        merge_kernel,
        out_shape=[jax.ShapeDtypeStruct(up.shape, up.dtype)] * 2,
        in_specs=[vmem] * 4,
        out_specs=[vmem] * 2,
        compiler_params=pltpu.CompilerParams(vmem_limit_bytes=8 * MIB),
        cost_estimate=pl.CostEstimate(flops=0, bytes_accessed=MIB, transcendentals=0),
    )(up, down, top, low)


def final_kernel(suffix, chunks, order, *refs):
    o_ref = refs[-1]
    for lo, at in chunks:
        terms = refs[at : at + 3]

        @pl.loop(0, terms[0].shape[0] // suffix)
        def _(n, lo=lo, terms=terms):
            here = pl.ds(pl.multiple_of(n * suffix, suffix), suffix)
            total = sum(term[here].astype(jnp.float32) for term in terms)
            o_ref[order[lo + n]] = total.astype(jnp.bfloat16)


class Projection:
    def __init__(self, place, w_out, mine, width, *tokens):
        near = project_other(place, mine, w_out, (2,), width)
        near, *self.tokens = together(near, *tokens)
        self.near = swap_core(near)
        self.project = functools.partial(project_own, place, mine, w_out)
        self.top2, self.low2 = self.project((2,), self.near, 0, True)
        later, _ = together(mine, near)
        self.rest = swap_core(project_other(place, later, w_out, (1, 3, 0), width))

    def across(self):
        return send_y(self.top2, 1), send_y(self.low2, -1)

    def beside(self):
        return self.project((1, 3), self.rest, 0)

    def own(self):
        return self.project((0,), self.rest, 2)[0]


def shards(queries, prefix_kv, suffix_kv, candidate_prefix, w_out):
    count, suffix, width = queries.shape
    length = prefix_kv.shape[2]
    out_width = w_out.shape[1] // (2 * NY)
    chunk = count - 2 * LATE
    others = count - chunk
    order, codes, info = plan(candidate_prefix)

    gather = Gather(prefix_kv.reshape(2, length, HD))
    (order, codes, info), sources = gather.early(order, codes, info)

    mine = attend(order, codes, queries, suffix_kv, sources, 0, chunk, length)
    gather.late()
    mine = mine.reshape(chunk * suffix, width)
    gather.last(mine)
    one = Projection(info, w_out, mine, out_width)
    top2, low2 = one.across()
    up, down = one.beside()
    (up, down, top2, low2, order2), sources = gather.finish(up, down, top2, low2, order)
    up, down = merge(up, down, top2, low2)
    up, down = send_y(up, 1), send_y(down, -1)

    mine = attend(order2, codes, queries, suffix_kv, sources, chunk, others, length)
    two = Projection(info, w_out, mine.reshape(others * suffix, width), out_width, up, down)
    up, down = two.tokens
    terms = [one.own(), up, down]
    top2, low2 = two.across()
    up, down = two.beside()
    up, down = merge(up, down, top2, low2)
    terms += [two.own(), send_y(up, 1), send_y(down, -1)]
    return pl.pallas_call(
        functools.partial(final_kernel, suffix, [(0, 0), (chunk, 3)]),
        out_shape=jax.ShapeDtypeStruct((count, suffix, out_width), jnp.bfloat16),
        in_specs=[pl.BlockSpec(memory_space=pltpu.SMEM)]
        + [pl.BlockSpec(memory_space=pltpu.VMEM)] * 6,
        out_specs=pl.BlockSpec(memory_space=pltpu.VMEM),
        compiler_params=pltpu.CompilerParams(vmem_limit_bytes=12 * MIB),
    )(order, *terms)


def solution(mesh):
    in_specs = (
        P("cache", None, "tensor"),
        P(None, "cache", None, "tensor"),
        P(None, "cache", None, "tensor"),
        P("cache", None),
        P("tensor", None),
    )
    out_specs = P("cache", None, "tensor")
    return jax.shard_map(shards, mesh=mesh, in_specs=in_specs, out_specs=out_specs, check_vma=False)
```

```python
import functools
import math

import jax
import jax.numpy as jnp
from jax import lax
from jax.experimental import pallas as pl
from jax.experimental.pallas import tpu as pltpu
from jax.sharding import PartitionSpec as P

H = 64
KVH = 8
HD = 128
GROUP = H // KVH
NX = 4
NZ = 8
NY = 4
LATE = 9
LOG2E = 1.4426950408889634
MIB = 1024 * 1024


def send_cache(value, along_z):
    pairs = []
    for x in range(NX):
        for z in range(NZ):
            for t in range(2 * NY):
                step = -1 if t % 2 else 1
                to_x, to_z = (x, (z + step) % NZ) if along_z else ((x + step) % NX, z)
                pairs.append(((x * NZ + z) * 2 * NY + t, (to_x * NZ + to_z) * 2 * NY + t))
    return lax.ppermute(value, ("cache", "tensor"), pairs)


def send_y(value, step):
    pairs = [(2 * y + c, 2 * ((y + step) % NY) + c) for y in range(NY) for c in range(2)]
    return lax.ppermute(value, "tensor", pairs)


def swap_core(value):
    return lax.ppermute(value, "tensor", [(t, t ^ 1) for t in range(2 * NY)])


def together(*values):
    return lax.optimization_barrier(values)


def pack_kernel(places, n_arrays, *refs):
    o_ref = refs[n_arrays]
    for index, (which, at) in places:
        o_ref[index] = refs[which][at]


def pack(parts):
    arrays = []
    places = []
    for i, row in enumerate(parts):
        for j, (array, at) in enumerate(row):
            which = next((n for n, a in enumerate(arrays) if a is array), len(arrays))
            if which == len(arrays):
                arrays.append(array)
            places.append(((i, j), (which, at)))
    block = arrays[0].shape[-2:]
    vmem = pl.BlockSpec(memory_space=pltpu.VMEM)
    return pl.pallas_call(
        functools.partial(pack_kernel, places, len(arrays)),
        out_shape=jax.ShapeDtypeStruct((len(parts), len(parts[0])) + block, jnp.bfloat16),
        in_specs=[vmem] * len(arrays),
        out_specs=vmem,
        compiler_params=pltpu.CompilerParams(vmem_limit_bytes=6 * MIB),
        cost_estimate=pl.CostEstimate(flops=0, bytes_accessed=MIB, transcendentals=0),
    )(*arrays)


class Gather:
    def __init__(self, block):
        self.block = block
        self.sources = {}

    def part(self, array, at, kv, dz, dx):
        code = (dz % NZ) * NX + dx % NX
        self.sources.setdefault(code, []).append((array, at, kv))

    def whole(self, array, at, dz, dx):
        for kv in range(2):
            self.part(array, at + (kv,), kv, dz, dx)

    def early(self, *tokens):
        block = self.block
        other = swap_core(block)
        both = pack([[(block, 0), (block, 1)], [(other, 0), (other, 1)]])
        x1, z1 = send_cache(both, False), send_cache(both, True)
        x1, z1, *tokens = together(x1, z1, *tokens)
        x1m, z1m = swap_core(x1), swap_core(z1)
        x2, z2 = send_cache(x1, False), send_cache(z1, True)
        x2, z2, x1m, z1m = together(x2, z2, x1m, z1m)
        values = pack(
            [
                [(x1, (0, 1)), (x1m, (1, 1)), (x2, (0, 1))],
                [(x1, (1, 1)), (x1m, (0, 1)), (x2, (1, 1))],
            ]
        )
        z2m = swap_core(z2)
        near = pack(
            [
                [(z1, (0, 0)), (z1m, (1, 0)), (z2, (0, 0)), (z2m, (1, 0))],
                [(z1, (1, 0)), (z1m, (0, 0)), (z2, (1, 0)), (z2m, (0, 0))],
            ]
        )
        v1, n1 = send_cache(values, True), send_cache(near, False)
        z3 = send_cache(z2, True)
        v1, n1, z3 = together(v1, n1, z3)
        z3m, n1m, v1m = swap_core(z3), swap_core(n1[1]), swap_core(v1[1])
        z4, n2, v2 = send_cache(z3[0], True), send_cache(n1[0], False), send_cache(v1, True)
        z4, n2, v2, z3m, n1m, v1m = together(z4, n2, v2, z3m, n1m, v1m)
        v2m = swap_core(v2[1])

        self.whole(block, (), 0, 0)
        self.whole(x1, (0,), 0, 1)
        self.whole(x1m, (1,), 0, -1)
        self.whole(x2, (0,), 0, 2)
        for step, mine, mate in ((1, z1, z1m), (2, z2, z2m), (3, z3, z3m)):
            self.whole(mine, (0,), step, 0)
            self.whole(mate, (1,), -step, 0)
        self.whole(z4, (), 4, 0)
        for step, mine, mate in ((1, v1, v1m), (2, v2, v2m)):
            self.values(mine, mate, step)
        for at, dz in enumerate((1, -1, 2, -2)):
            self.part(n1, (0, at), 0, dz, 1)
            self.part(n1m, (at,), 0, -dz, -1)
            self.part(n2, (at,), 0, dz, 2)
        self.left = v2, z3, z3m, z4
        return tokens, {code: list(parts) for code, parts in self.sources.items()}

    def values(self, mine, mate, step):
        for at, dx in enumerate((1, -1, 2)):
            self.part(mine, (0, at), 1, step, dx)
            self.part(mate, (at,), 1, -step, -dx)

    def late(self):
        v2, z3, z3m, z4 = self.left
        key_z4m = swap_core(z4[0:1])
        distant = pack(
            [
                [(z3, (0, 0)), (z3m, (1, 0)), (z4, 0)],
                [(z3, (1, 0)), (z3m, (0, 0)), (key_z4m, 0)],
            ]
        )
        self.hop = send_cache(v2, True), send_cache(distant, False)

    def last(self, token):
        token, v3, f1 = together(token, *self.hop)
        v4, f2 = send_cache(v3[0], True), send_cache(f1[0], False)
        self.final = v3, f1, v4, f2
        return token

    def finish(self, *tokens):
        count = len(tokens)
        done = together(*tokens, *self.final)
        v3, f1, v4, f2 = done[count:]
        third = range(3)
        rest = swap_core(pack([[(v3, (1, at)) for at in third], [(f1, (1, at)) for at in third]]))
        for at, dx in enumerate((1, -1, 2)):
            self.part(v3, (0, at), 1, 3, dx)
            self.part(rest, (0, at), 1, -3, -dx)
            self.part(v4, (at,), 1, 4, dx)
        for at, dz in enumerate((3, -3, 4)):
            self.part(f1, (0, at), 0, dz, 1)
            self.part(rest, (1, at), 0, -dz, -1)
            self.part(f2, (at,), 0, dz, 2)
        return done[:count], self.sources


LAST = (((1,), (1,)), ((), ()))
INNER = (((1,), (0,)), ((), ()))


def beside_ones(values):
    return jnp.concatenate([values, jnp.ones_like(values)], axis=1)


def plan_kernel(ids, order, codes, info):
    me = lax.axis_index("cache")
    t = lax.axis_index("tensor")
    count = ids.shape[0]
    info[0] = t // 2
    info[1] = t % 2

    def is_early(code):
        dz = code // NX
        return (code % NX == 0) | (dz <= 2) | (dz >= NZ - 2)

    def first(n, at):
        passage = ids[n]
        dz = (passage % NZ - me % NZ + NZ) % NZ
        dx = (passage // NZ - me // NZ + NX) % NX
        dz = jnp.where(t % 2 == 0, (NZ - dz) % NZ, dz)
        dx = jnp.where(t % 2 == 0, (NX - dx) % NX, dx)
        code = dz * NX + dx
        codes[n] = code
        order[at] = n
        return at + is_early(code).astype(jnp.int32)

    early = lax.fori_loop(0, count, first, jnp.int32(0))

    def second(n, at):
        late = jnp.logical_not(is_early(codes[n]))

        @pl.when(late)
        def _():
            order[at] = n

        return at + late.astype(jnp.int32)

    lax.fori_loop(0, count, second, early)


def plan(candidate_prefix):
    count = candidate_prefix.shape[0]
    smem = pl.BlockSpec(memory_space=pltpu.SMEM)
    return pl.pallas_call(
        plan_kernel,
        out_shape=[jax.ShapeDtypeStruct((n,), jnp.int32) for n in (count, count, 2)],
        in_specs=[smem],
        out_specs=[smem] * 3,
        compiler_params=pltpu.CompilerParams(vmem_limit_bytes=MIB),
        cost_estimate=pl.CostEstimate(flops=1000, bytes_accessed=1000, transcendentals=0),
    )(candidate_prefix.reshape(count))


def attention_kernel(sources, n_arrays, lo, count, batch, order, codes, q_ref, s_ref, *rest):
    arrays = rest[:n_arrays]
    o_ref, cache = rest[n_arrays:]
    suffix = q_ref.shape[1]
    rows = GROUP * suffix
    factor = LOG2E / math.sqrt(HD)
    token = lax.broadcasted_iota(jnp.int32, (rows, HD), 0) % suffix
    causal = lax.broadcasted_iota(jnp.int32, (rows, HD), 1) <= token
    blank = jnp.zeros((HD - suffix, HD), jnp.bfloat16)

    def fetch(first):
        @pl.loop(0, batch)
        def _(i):
            code = codes[order[first + i]]
            for dx in range(NX):

                @pl.when(code % NX == dx)
                def _(dx=dx):
                    for dz in range(NZ):
                        parts = sources.get(dz * NX + dx)
                        if parts is None:
                            continue

                        @pl.when(code // NX == dz)
                        def _(parts=parts):
                            for which, at, kv in parts:
                                cache[i, kv] = arrays[which][at]

    def attend_batch(first, at):
        fetch(first)
        scores = []
        for i in range(batch):
            n = order[first + i]
            q = jnp.concatenate([q_ref[n, :, g * HD : (g + 1) * HD] for g in range(GROUP)], axis=0)
            far = lax.dot_general(q, cache[i, 0], LAST, preferred_element_type=jnp.float32)
            keys = jnp.concatenate([s_ref[0, n], blank], axis=0)
            near = lax.dot_general(q, keys, LAST, preferred_element_type=jnp.float32)
            near = jnp.where(causal, near, -jnp.inf)
            scores.append([far[:, j : j + HD] for j in range(0, far.shape[1], HD)] + [near])
        weights = []
        for tiles in scores:
            top = jnp.max(functools.reduce(jnp.maximum, tiles), axis=1, keepdims=True)
            weights.append([jnp.exp2((s - top) * factor).astype(jnp.bfloat16) for s in tiles])
        for i in range(batch):
            n = order[first + i]
            far = jnp.concatenate(weights[i][:-1], axis=1)
            near = weights[i][-1][:, :suffix]
            summed = lax.dot_general(
                far, beside_ones(cache[i, 1]), INNER, preferred_element_type=jnp.float32
            ) + lax.dot_general(
                near, beside_ones(s_ref[1, n]), INNER, preferred_element_type=jnp.float32
            )
            result = (summed[:, :HD] / summed[:, HD:]).astype(jnp.bfloat16)
            for g in range(GROUP):
                o_ref[at + i, :, g * HD : (g + 1) * HD] = result[g * suffix : (g + 1) * suffix]

    @pl.loop(0, -(-count // batch))
    def _(step):
        at = jnp.minimum(step * batch, count - batch)
        attend_batch(lo + at, at)


def attend(order, codes, queries, suffix_kv, sources, lo, count, length):
    arrays = []
    places = {}
    for code, parts in sources.items():
        for array, at, kv in parts:
            which = next((n for n, a in enumerate(arrays) if a is array), len(arrays))
            if which == len(arrays):
                arrays.append(array)
            places.setdefault(code, []).append((which, at, kv))
    _, suffix, width = queries.shape
    batch = max(n for n in range(1, 8) if count % n == 0)
    vmem = pl.BlockSpec(memory_space=pltpu.VMEM)
    smem = pl.BlockSpec(memory_space=pltpu.SMEM)
    shape = jax.ShapeDtypeStruct((count, suffix, width), jnp.bfloat16)
    return pl.pallas_call(
        functools.partial(attention_kernel, places, len(arrays), lo, count, batch),
        out_shape=shape,
        in_specs=[smem] * 2 + [vmem] * (2 + len(arrays)),
        out_specs=vmem,
        scratch_shapes=[pltpu.VMEM((batch, 2, length, HD), jnp.bfloat16)],
        compiler_params=pltpu.CompilerParams(vmem_limit_bytes=28 * MIB),
        cost_estimate=pl.CostEstimate(
            flops=4 * count * suffix * width * length,
            bytes_accessed=8 * MIB,
            transcendentals=count * suffix * GROUP * length,
        ),
    )(order, codes, queries, suffix_kv, *arrays)


def columns_of(place, turn, other, width):
    core = 1 - place[1] if other else place[1]
    return pl.multiple_of((2 * lax.rem(place[0] + turn, NY) + core) * width, width)


def project_other_kernel(turns, place, a_ref, w_ref, o_ref):
    width = o_ref.shape[2]
    for at, turn in enumerate(turns):
        column = columns_of(place, turn, True, width)
        total = jnp.dot(
            a_ref[...], w_ref[:, pl.ds(column, width)], preferred_element_type=jnp.float32
        )
        o_ref[at] = total.astype(jnp.bfloat16)


def project_own_kernel(turns, first, split, place, a_ref, w_ref, came_ref, *outs):
    width = came_ref.shape[2]
    half = a_ref.shape[0] // 2
    for at, turn in enumerate(turns):
        column = columns_of(place, turn, False, width)
        total = jnp.dot(
            a_ref[...], w_ref[:, pl.ds(column, width)], preferred_element_type=jnp.float32
        )
        total = (total + came_ref[first + at].astype(jnp.float32)).astype(jnp.bfloat16)
        if split:
            outs[2 * at][...] = total[:half]
            outs[2 * at + 1][...] = total[half:]
        else:
            outs[at][...] = total


def project(kernel, out_shape, place, *arrays):
    vmem = pl.BlockSpec(memory_space=pltpu.VMEM)
    rows, depth = arrays[0].shape
    outs = out_shape if isinstance(out_shape, list) else [out_shape]
    size = sum(math.prod(out.shape) for out in outs)
    return pl.pallas_call(
        kernel,
        out_shape=out_shape,
        in_specs=[pl.BlockSpec(memory_space=pltpu.SMEM)] + [vmem] * len(arrays),
        out_specs=[vmem] * len(outs) if isinstance(out_shape, list) else vmem,
        compiler_params=pltpu.CompilerParams(vmem_limit_bytes=20 * MIB),
        cost_estimate=pl.CostEstimate(
            flops=2 * size * depth, bytes_accessed=4 * MIB, transcendentals=0
        ),
    )(place, *arrays)


def project_other(place, mine, w_out, turns, width):
    shape = jax.ShapeDtypeStruct((len(turns), mine.shape[0], width), jnp.bfloat16)
    return project(functools.partial(project_other_kernel, turns), shape, place, mine, w_out)


def project_own(place, mine, w_out, turns, came, first, split=False):
    parts = 2 if split else 1
    shape = jax.ShapeDtypeStruct((mine.shape[0] // parts, came.shape[2]), jnp.bfloat16)
    kernel = functools.partial(project_own_kernel, turns, first, split)
    return project(kernel, [shape] * (parts * len(turns)), place, mine, w_out, came)


def merge_kernel(up, down, top, low, up_out, down_out):
    half = top.shape[0]
    up_out[:half] = (up[:half].astype(jnp.float32) + top[...]).astype(jnp.bfloat16)
    up_out[half:] = up[half:]
    down_out[:half] = down[:half]
    down_out[half:] = (down[half:].astype(jnp.float32) + low[...]).astype(jnp.bfloat16)


def merge(up, down, top, low):
    vmem = pl.BlockSpec(memory_space=pltpu.VMEM)
    return pl.pallas_call(
        merge_kernel,
        out_shape=[jax.ShapeDtypeStruct(up.shape, up.dtype)] * 2,
        in_specs=[vmem] * 4,
        out_specs=[vmem] * 2,
        compiler_params=pltpu.CompilerParams(vmem_limit_bytes=8 * MIB),
        cost_estimate=pl.CostEstimate(flops=0, bytes_accessed=MIB, transcendentals=0),
    )(up, down, top, low)


def final_kernel(suffix, chunks, order, *refs):
    o_ref = refs[-1]
    for lo, at in chunks:
        terms = refs[at : at + 3]

        @pl.loop(0, terms[0].shape[0] // suffix)
        def _(n, lo=lo, terms=terms):
            here = pl.ds(pl.multiple_of(n * suffix, suffix), suffix)
            total = sum(term[here].astype(jnp.float32) for term in terms)
            o_ref[order[lo + n]] = total.astype(jnp.bfloat16)


class Projection:
    def __init__(self, place, w_out, mine, width, *tokens):
        near = project_other(place, mine, w_out, (2,), width)
        near, *self.tokens = together(near, *tokens)
        self.near = swap_core(near)
        self.project = functools.partial(project_own, place, mine, w_out)
        self.top2, self.low2 = self.project((2,), self.near, 0, True)
        later, _ = together(mine, near)
        self.rest = swap_core(project_other(place, later, w_out, (1, 3, 0), width))

    def across(self):
        return send_y(self.top2, 1), send_y(self.low2, -1)

    def beside(self):
        return self.project((1, 3), self.rest, 0)

    def own(self):
        return self.project((0,), self.rest, 2)[0]


def shards(queries, prefix_kv, suffix_kv, candidate_prefix, w_out):
    count, suffix, width = queries.shape
    length = prefix_kv.shape[2]
    out_width = w_out.shape[1] // (2 * NY)
    chunk = count - 2 * LATE
    others = count - chunk
    order, codes, info = plan(candidate_prefix)

    gather = Gather(prefix_kv.reshape(2, length, HD))
    (order, codes, info), sources = gather.early(order, codes, info)

    mine = attend(order, codes, queries, suffix_kv, sources, 0, chunk, length)
    gather.late()
    mine = mine.reshape(chunk * suffix, width)
    gather.last(mine)
    one = Projection(info, w_out, mine, out_width)
    top2, low2 = one.across()
    up, down = one.beside()
    (up, down, top2, low2, order2), sources = gather.finish(up, down, top2, low2, order)
    up, down = merge(up, down, top2, low2)
    up, down = send_y(up, 1), send_y(down, -1)

    mine = attend(order2, codes, queries, suffix_kv, sources, chunk, others, length)
    two = Projection(info, w_out, mine.reshape(others * suffix, width), out_width, up, down)
    up, down = two.tokens
    terms = [one.own(), up, down]
    top2, low2 = two.across()
    up, down = two.beside()
    up, down = merge(up, down, top2, low2)
    terms += [two.own(), send_y(up, 1), send_y(down, -1)]
    return pl.pallas_call(
        functools.partial(final_kernel, suffix, [(0, 0), (chunk, 3)]),
        out_shape=jax.ShapeDtypeStruct((count, suffix, out_width), jnp.bfloat16),
        in_specs=[pl.BlockSpec(memory_space=pltpu.SMEM)]
        + [pl.BlockSpec(memory_space=pltpu.VMEM)] * 6,
        out_specs=pl.BlockSpec(memory_space=pltpu.VMEM),
        compiler_params=pltpu.CompilerParams(vmem_limit_bytes=12 * MIB),
    )(order, *terms)


def solution(mesh):
    in_specs = (
        P("cache", None, "tensor"),
        P(None, "cache", None, "tensor"),
        P(None, "cache", None, "tensor"),
        P("cache", None),
        P("tensor", None),
    )
    out_specs = P("cache", None, "tensor")
    return jax.shard_map(shards, mesh=mesh, in_specs=in_specs, out_specs=out_specs, check_vma=False)
```
